128 devices in a mesh: store: 4 (over z), tile: 32 (over y, x, core).
Axes of the slice: x: 4, y: 4, z: 4, core: 2. Of those that a mesh axis runs over, the one named last changes fastest.
Arguments:
- embeddings: bfloat16 [65536, 1024], P(('store', 'tile')), may hold values from -8 to 8
- member_rows: int32 [65536], replicated, may hold values from 0 to 65535, as said below
- cluster_sizes: int32 [8], replicated, may hold values from 2048 to 14336, as said below
- unit_pairs: int32 [128, 1, 3], replicated, may hold values from -1 to 7, as said below
Outputs:
- best_similarity: float32 [65536], P(('store', 'tile'))
The draws below stay inside these ranges and needn't reach their ends.
Inputs may be any that keep to these rules, and one draw needn't show every extreme that they name: `member_rows`: A permutation of the row ids; clusters lie one after another in this order. Each aligned block of 256 positions holds exactly 2 rows of each device's 512 consecutive row ids. `cluster_sizes`: multiples of 2048 that sum to 65536. `unit_pairs`: each entry is (c, i, j) with i <= j < cluster_sizes[c] // 2048, or (-1, -1, -1) for an empty slot; every such pair of groups of every cluster appears exactly once.
All inputs are finite; a program needn't handle non-finite values.
Results may differ from the reference program's by a relative error of at most 0.00042.
Values may be sent and summed in bfloat16 or wider, within the bound.
A program may use at most 64 MiB of HBM per device.

```python
import math
import jax
import jax.numpy as jnp
import numpy as np
from jax import lax

D = 1024
BLOCK = 256
GROUP_BLOCKS = 8
MOST_GROUPS = 7
ROWS_DEV = 512
OWNERS = 128
ROWS = 65536
NCLUST = 8
UNITS_DEV = 1
N_STORE = 4
N_TILE = 32


def structure(key):
    devices = N_STORE * N_TILE
    per_block = BLOCK // devices
    block_count = ROWS // BLOCK
    group_rows = BLOCK * GROUP_BLOCKS
    key_local, key_slot, key_size, key_order, key_owner = jax.random.split(key, 5)
    local_perm = jax.vmap(lambda part_key: jax.random.permutation(part_key, ROWS_DEV))(jax.random.split(key_local, devices))
    slot_perm = jax.vmap(lambda part_key: jax.random.permutation(part_key, BLOCK))(jax.random.split(key_slot, block_count))
    storage = slot_perm // per_block
    within = slot_perm % per_block
    block_base = jnp.arange(block_count, dtype=jnp.int32)[:, None] * per_block
    local_row = local_perm[storage, block_base + within]
    member_rows = (storage * ROWS_DEV + local_row).reshape(ROWS).astype(jnp.int32)
    half_count = NCLUST // 2
    shifts = jax.random.randint(key_size, (half_count,), -3, 4).astype(jnp.int32)
    shifts = shifts.at[0].set(3)
    paired = jnp.stack([4 + shifts, 4 - shifts], axis=1).reshape(NCLUST)
    group_counts = paired[jax.random.permutation(key_order, NCLUST)]
    cluster_sizes = (group_counts * group_rows).astype(jnp.int32)
    low_index, high_index = np.triu_indices(MOST_GROUPS)
    pair_count = low_index.shape[0]
    cand_cluster = jnp.repeat(jnp.arange(NCLUST, dtype=jnp.int32), pair_count)
    cand_low = jnp.tile(jnp.asarray(low_index, jnp.int32), NCLUST)
    cand_high = jnp.tile(jnp.asarray(high_index, jnp.int32), NCLUST)
    usable = cand_high < group_counts[cand_cluster]
    sort_order = jnp.argsort(jnp.where(usable, 0, 1).astype(jnp.int32), stable=True)
    slot_total = OWNERS * UNITS_DEV
    chosen = sort_order[:slot_total]
    kept = usable[chosen]
    triples = jnp.stack([jnp.where(kept, cand_cluster[chosen], -1), jnp.where(kept, cand_low[chosen], -1), jnp.where(kept, cand_high[chosen], -1)], axis=1).astype(jnp.int32)
    placed = jnp.zeros((slot_total, 3), jnp.int32).at[jax.random.permutation(key_owner, slot_total)].set(triples)
    return (member_rows, cluster_sizes, placed.reshape(OWNERS, UNITS_DEV, 3))


def draw_member_rows(key, part):
    return structure(key)[0]


def draw_cluster_sizes(key, part):
    return structure(key)[1]


def draw_unit_pairs(key, part):
    return structure(key)[2]


def draw_embeddings(key, part):
    member_rows, cluster_sizes, unit_pairs = structure(key)
    key = jax.random.fold_in(key, 7)
    key_center, key_weight, key_noise, key_scale = jax.random.split(key, 4)
    ends = jnp.cumsum(cluster_sizes)
    positions = jnp.arange(ROWS, dtype=jnp.int32)
    position_cluster = jnp.sum((positions[:, None] >= ends[None, :]).astype(jnp.int32), axis=1)
    row_cluster = jnp.zeros((ROWS,), jnp.int32).at[member_rows].set(position_cluster)
    centers = jax.random.normal(key_center, (NCLUST, D), jnp.float32)
    weights = jax.random.uniform(key_weight, (NCLUST, 1), jnp.float32, 0.3, 1.5)
    row_scale = jnp.exp(jax.random.uniform(key_scale, (ROWS, 1), jnp.float32, math.log(0.25), math.log(4.0)))
    noise = jax.random.normal(key_noise, (ROWS, D), jnp.float32)
    values = (weights * centers)[row_cluster] + row_scale * noise
    return jnp.clip(values, -8.0, 8.0).astype(jnp.bfloat16)


def setup_inputs(seed: int = 0) -> dict:
    streams_of = jax.random.split(jax.random.key(seed), 5)
    embeddings = draw_embeddings(jax.random.fold_in(streams_of[4], 71), 0)
    member_rows = draw_member_rows(jax.random.fold_in(streams_of[4], 71), 0)
    cluster_sizes = draw_cluster_sizes(jax.random.fold_in(streams_of[4], 71), 0)
    unit_pairs = draw_unit_pairs(jax.random.fold_in(streams_of[4], 71), 0)
    return dict(embeddings=embeddings, member_rows=member_rows, cluster_sizes=cluster_sizes, unit_pairs=unit_pairs)


EPS = 1e-06
FLOOR = -4.0

def reference(embeddings, member_rows, cluster_sizes, unit_pairs):
    group_rows = BLOCK * GROUP_BLOCKS
    total_rows = member_rows.shape[0]
    widened = embeddings.astype(jnp.float32)
    squares = lax.optimization_barrier(jnp.sum(widened * widened, axis=1, keepdims=True))
    unit_rows = (widened * lax.rsqrt(squares + EPS)).astype(jnp.bfloat16)
    ordered = unit_rows[member_rows]
    starts = (jnp.cumsum(cluster_sizes) - cluster_sizes).astype(jnp.int32)
    flat_units = unit_pairs.reshape(-1, 3)
    offsets = jnp.arange(group_rows, dtype=jnp.int32)

    def one_unit(triple):
        usable = triple[0] >= 0
        cluster = jnp.maximum(triple[0], 0)
        left_first = (starts[cluster] + jnp.maximum(triple[1], 0) * group_rows).astype(jnp.int32)
        right_first = (starts[cluster] + jnp.maximum(triple[2], 0) * group_rows).astype(jnp.int32)
        left_rows = lax.dynamic_slice_in_dim(ordered, left_first, group_rows)
        right_rows = lax.dynamic_slice_in_dim(ordered, right_first, group_rows)
        scores = jnp.dot(left_rows, right_rows.T, preferred_element_type=jnp.float32)
        same = (left_first + offsets)[:, None] == (right_first + offsets)[None, :]
        scores = jnp.where(same, FLOOR, scores)
        row_best = jnp.where(usable, lax.optimization_barrier(jnp.max(scores, axis=1)), FLOOR)
        col_best = jnp.where(usable, lax.optimization_barrier(jnp.max(scores, axis=0)), FLOOR)
        return (row_best, col_best, left_first + offsets, right_first + offsets)
    row_best, col_best, left_pos, right_pos = lax.map(one_unit, flat_units)
    best_pos = jnp.full((total_rows,), FLOOR, jnp.float32)
    best_pos = best_pos.at[left_pos.reshape(-1)].max(row_best.reshape(-1))
    best_pos = best_pos.at[right_pos.reshape(-1)].max(col_best.reshape(-1))
    return jnp.zeros((total_rows,), jnp.float32).at[member_rows].set(best_pos)
```

```python
import jax
import jax.numpy as jnp
from jax import lax
from jax.sharding import PartitionSpec as P

BLOCK = 256
GROUP_BLOCKS = 8
GROUP = BLOCK * GROUP_BLOCKS
AXES = ("store", "tile")
EPS = 1e-06
FLOOR = -4.0


def compare_pair(left, right, same_group):
    span = 512

    def step(col_best, at):
        part = lax.dynamic_slice_in_dim(left, at, span)
        scores = lax.dot_general(part, right, (((1,), (1,)), ((), ())), preferred_element_type=jnp.float32)
        row_ids = at + lax.broadcasted_iota(jnp.int32, scores.shape, 0)
        col_ids = lax.broadcasted_iota(jnp.int32, scores.shape, 1)
        scores = jnp.where((row_ids == col_ids) & same_group, FLOOR, scores)
        return jnp.maximum(col_best, jnp.max(scores, axis=0)), jnp.max(scores, axis=1)

    first = jnp.full((right.shape[0],), FLOOR, jnp.float32)
    col_best, row_best = lax.scan(step, first, jnp.arange(0, left.shape[0], span, dtype=jnp.int32))
    return row_best.reshape(-1), col_best


def shards(embeddings, member_rows, cluster_sizes, unit_pairs):
    devices = lax.axis_size(AXES)
    me = lax.axis_index(AXES)
    rows_dev, width = embeddings.shape
    groups = member_rows.shape[0] // GROUP
    share = GROUP // devices
    owners = unit_pairs.shape[0]

    wide = embeddings.astype(jnp.float32)
    squares = jnp.sum(jnp.square(wide), axis=1, keepdims=True)
    unit = (wide * lax.rsqrt(squares + EPS)).astype(jnp.bfloat16)

    local = member_rows.reshape(-1, BLOCK) - me * rows_dev
    mine = (local >= 0) & (local < rows_dev)
    low = jnp.min(jnp.where(mine, local, rows_dev), axis=1)
    high = jnp.max(jnp.where(mine, local, -1), axis=1)
    order = jnp.stack([low, high], axis=1).reshape(rows_dev)
    pick = order[:, None] == jnp.arange(rows_dev, dtype=jnp.int32)[None, :]
    ordered = lax.dot_general(
        pick.astype(jnp.bfloat16), unit, (((1,), (0,)), ((), ())), preferred_element_type=jnp.float32
    ).astype(jnp.bfloat16)
    by_group = ordered.reshape(groups, share, width)

    first_group = (jnp.cumsum(cluster_sizes) - cluster_sizes) // GROUP
    pairs = unit_pairs[:, 0]
    usable = pairs[:, 0] >= 0
    sides = first_group[jnp.maximum(pairs[:, :1], 0)] + jnp.maximum(pairs[:, 1:], 0)
    outgoing = by_group[sides].reshape(owners, 2 * share, width)
    arrived = lax.all_to_all(outgoing, AXES, split_axis=0, concat_axis=0, tiled=True)
    arrived = arrived.reshape(devices, 2, share, width)
    left = arrived[:, 0].reshape(GROUP, width)
    right = arrived[:, 1].reshape(GROUP, width)
    row_best, col_best = compare_pair(left, right, sides[me, 0] == sides[me, 1])
    best = jnp.stack([row_best.reshape(devices, share), col_best.reshape(devices, share)], axis=1)
    best = jnp.where(usable[me], best, FLOOR).reshape(devices, 2 * share)
    back = lax.all_to_all(best, AXES, split_axis=0, concat_axis=0, tiled=True)
    back = back.reshape(owners * 2, share)
    of_group = sides.reshape(-1)[None, :] == jnp.arange(groups, dtype=jnp.int32)[:, None]
    best_slot = jnp.max(jnp.where(of_group[:, :, None], back[None], FLOOR), axis=1)
    return jnp.max(jnp.where(pick, best_slot.reshape(rows_dev, 1), FLOOR), axis=0)


def solution(mesh):
    placed = (P(AXES, None), P(), P(), P())
    return jax.shard_map(shards, mesh=mesh, in_specs=placed, out_specs=P(AXES), check_vma=False)
```

```python
import functools

import jax
import jax.numpy as jnp
from jax import lax
from jax.experimental import pallas as pl
from jax.experimental.pallas import tpu as pltpu
from jax.sharding import PartitionSpec as P

BLOCK = 256
GROUP_BLOCKS = 8
GROUP = BLOCK * GROUP_BLOCKS
AXES = ("store", "tile")
EPS = 1e-06
FLOOR = -4.0

MESH = pl.DeviceIdType.MESH
PLANES = 4
SIDE = 4
SLOTS = 8
SHARE = 16
PIECE = 8 * SHARE
CHUNK = SIDE * PIECE
D = 1024
BF16 = jnp.bfloat16
F32 = jnp.float32
I32 = jnp.int32


def compare_pair(left, right, same_group):
    span = 512

    def step(col_best, at):
        part = lax.dynamic_slice_in_dim(left, at, span)
        scores = lax.dot_general(part, right, (((1,), (1,)), ((), ())), preferred_element_type=F32)
        row_ids = at + lax.broadcasted_iota(I32, scores.shape, 0)
        col_ids = lax.broadcasted_iota(I32, scores.shape, 1)
        scores = jnp.where((row_ids == col_ids) & same_group, FLOOR, scores)
        return jnp.maximum(col_best, jnp.max(scores, axis=0)), jnp.max(scores, axis=1)

    first = jnp.full((right.shape[0],), FLOOR, F32)
    col_best, row_best = lax.scan(step, first, jnp.arange(0, left.shape[0], span, dtype=I32))
    return row_best.reshape(-1), col_best


def direct(embeddings, member_rows, cluster_sizes, unit_pairs):
    devices = lax.axis_size(AXES)
    me = lax.axis_index(AXES)
    rows_dev, width = embeddings.shape
    groups = member_rows.size // GROUP
    share = GROUP // devices
    owners = unit_pairs.shape[0]

    wide = embeddings.astype(F32)
    squares = jnp.sum(jnp.square(wide), axis=1, keepdims=True)
    unit = (wide * lax.rsqrt(squares + EPS)).astype(BF16)

    local = member_rows.reshape(-1, BLOCK) - me * rows_dev
    mine = (local >= 0) & (local < rows_dev)
    low = jnp.min(jnp.where(mine, local, rows_dev), axis=1)
    high = jnp.max(jnp.where(mine, local, -1), axis=1)
    order = jnp.stack([low, high], axis=1).reshape(rows_dev)
    pick = order[:, None] == jnp.arange(rows_dev, dtype=I32)[None, :]
    ordered = lax.dot_general(
        pick.astype(BF16), unit, (((1,), (0,)), ((), ())), preferred_element_type=F32
    ).astype(BF16)
    by_group = ordered.reshape(groups, share, width)

    first_group = (jnp.cumsum(cluster_sizes) - cluster_sizes) // GROUP
    pairs = unit_pairs[:, 0]
    usable = pairs[:, 0] >= 0
    sides = first_group[jnp.maximum(pairs[:, :1], 0)] + jnp.maximum(pairs[:, 1:], 0)
    outgoing = by_group[sides].reshape(owners, 2 * share, width)
    arrived = lax.all_to_all(outgoing, AXES, split_axis=0, concat_axis=0, tiled=True)
    arrived = arrived.reshape(devices, 2, share, width)
    left = arrived[:, 0].reshape(GROUP, width)
    right = arrived[:, 1].reshape(GROUP, width)
    row_best, col_best = compare_pair(left, right, sides[me, 0] == sides[me, 1])
    best = jnp.stack([row_best.reshape(devices, share), col_best.reshape(devices, share)], axis=1)
    best = jnp.where(usable[me], best, FLOOR).reshape(devices, 2 * share)
    back = lax.all_to_all(best, AXES, split_axis=0, concat_axis=0, tiled=True)
    back = back.reshape(owners * 2, share)
    of_group = sides.reshape(-1)[None, :] == jnp.arange(groups, dtype=I32)[:, None]
    best_slot = jnp.max(jnp.where(of_group[:, :, None], back[None], FLOOR), axis=1)
    return jnp.max(jnp.where(pick, best_slot.reshape(rows_dev, 1), FLOOR), axis=0)


def prepare_kernel(clusters, sizes_ref, emb_ref, members_ref, rows_ref, ids_ref, clus_ref, fits_ref, group_at):
    me = lax.axis_index("store") * (2 * SIDE * SIDE) + lax.axis_index("tile")
    rows_dev = emb_ref.shape[0]
    counts = [sizes_ref[c] // GROUP for c in range(clusters)]
    way = lax.broadcasted_iota(I32, (128, 128), 0) * 128 + lax.broadcasted_iota(I32, (128, 128), 1)
    loads = jnp.full((128, 128), counts[0], I32)
    for c in range(1, clusters):
        plane = lax.shift_right_logical(way, 2 * (c - 1)) & 3
        loads += lax.shift_left(jnp.full((128, 128), counts[c], I32), plane * 8)
    most = loads & 255
    for p in range(1, PLANES):
        most = jnp.maximum(most, lax.shift_right_logical(loads, 8 * p) & 255)
    chosen = jnp.min(most * 16384 + way)
    fits_ref[0] = (chosen // 16384 <= SLOTS).astype(I32)
    groups = PLANES * SLOTS
    for d in range(groups):
        group_at[d] = 0
        clus_ref[d] = -1
    used = [jnp.int32(0)] * PLANES
    start = jnp.int32(0)
    for c in range(clusters):
        plane = jnp.int32(0) if c == 0 else lax.shift_right_logical(chosen, 2 * (c - 1)) & 3
        offset = jnp.int32(0)
        for p in range(PLANES):
            offset = jnp.where(plane == p, used[p], offset)

        def put(i, carry, c=c, plane=plane, offset=offset, start=start):
            at = jnp.minimum(plane * SLOTS + offset + i, groups - 1)
            group_at[at] = jnp.minimum(start + i, groups - 1)
            clus_ref[at] = c
            return carry

        lax.fori_loop(0, counts[c], put, 0)
        for p in range(PLANES):
            used[p] = jnp.where(plane == p, used[p] + counts[c], used[p])
        start = start + counts[c]

    def ids_of(d, carry):
        at = pl.multiple_of(group_at[d] * GROUP_BLOCKS, GROUP_BLOCKS)
        local = members_ref[pl.ds(at, GROUP_BLOCKS), :] - me * rows_dev
        mine = (local >= 0) & (local < rows_dev)
        low = jnp.min(jnp.where(mine, local, rows_dev), axis=1, keepdims=True)
        high = jnp.max(jnp.where(mine, local, -1), axis=1, keepdims=True)
        to = pl.multiple_of(d * SHARE, SHARE)
        ids_ref[pl.ds(to, 8), :] = jnp.broadcast_to(low, (8, 128))
        ids_ref[pl.ds(to + 8, 8), :] = jnp.broadcast_to(high, (8, 128))
        return carry

    lax.fori_loop(0, groups, ids_of, 0)
    wide = emb_ref[...].astype(F32)
    squares = jnp.sum(wide * wide, axis=1, keepdims=True)
    unit = (wide * lax.rsqrt(squares + EPS)).astype(BF16)
    pick = ids_ref[:, :1] == lax.broadcasted_iota(I32, (rows_dev, rows_dev), 1)
    picked = lax.dot_general(
        jnp.where(pick, 1.0, 0.0).astype(BF16), unit, (((1,), (0,)), ((), ())), preferred_element_type=F32
    )
    rows_ref[...] = picked.astype(BF16)


def prepare(embeddings, member_rows, cluster_sizes):
    rows_dev, width = embeddings.shape
    vmem = pl.BlockSpec(memory_space=pltpu.VMEM)
    smem = pl.BlockSpec(memory_space=pltpu.SMEM)
    groups = PLANES * SLOTS
    return pl.pallas_call(
        functools.partial(prepare_kernel, cluster_sizes.shape[0]),
        out_shape=(
            jax.ShapeDtypeStruct((rows_dev, width), BF16),
            jax.ShapeDtypeStruct((rows_dev, 128), I32),
            jax.ShapeDtypeStruct((groups,), I32),
            jax.ShapeDtypeStruct((1,), I32),
        ),
        in_specs=[smem, vmem, vmem],
        out_specs=(vmem, vmem, smem, smem),
        scratch_shapes=[pltpu.SMEM((groups,), I32)],
        compiler_params=pltpu.CompilerParams(vmem_limit_bytes=32 * 2**20),
        name="prepare",
    )(cluster_sizes, embeddings, member_rows.reshape(-1, BLOCK))


def plane_kernel(
    clus_ref, src, ids_ref, out_ref,
    zbuf, erow, ecol, fbuf, hbuf, racc, cacc, fcacc, fsend, hsend,
    rrow, rcol, brow, bcol, zout, fin,
    zs, zr, es, er, ec, gs, fr, hr, ss, sr,
    rs, rr, rc, bs, br, ts, tr,
):
    z = lax.axis_index("store")
    tile = lax.axis_index("tile")
    y, x, k = tile // 8, (tile // 2) % 4, tile % 2

    def dev(dz, dy, dx, dk):
        return (dz, dy * 8 + dx * 2 + dk)

    def row_first(cy, cx):
        step = lax.rem(cx - cy + 4, 4)
        return (step == 1) | ((step == 2) & (cy < 2))

    diagonal = y == x
    by_row = row_first(y, x)

    def copy(start, from_, to, ssem, rsem, dz, dy, dx, dk):
        mine = (dz == z) & (dy == y) & (dx == x) & (dk == k)
        far = pltpu.make_async_remote_copy(from_, to, ssem, rsem, device_id=dev(dz, dy, dx, dk), device_id_type=MESH)

        @pl.when(jnp.logical_not(mine))
        def _():
            if start:
                far.start()
            else:
                far.wait_send()

        if start:

            @pl.when(mine)
            def _():
                pltpu.make_async_copy(from_, to, rsem).start()

    def arrive(ref, sem):
        pltpu.make_async_copy(ref, ref, sem).wait()

    for ref in (rrow, rcol):
        ref[...] = jnp.full(ref.shape, FLOOR, F32)
    for ref in (racc, cacc, fcacc):
        ref[...] = jnp.full(ref.shape, FLOOR, F32)
    for ref in (fsend, hsend):
        ref[...] = jnp.full(ref.shape, FLOOR, F32)

    barrier = pltpu.get_barrier_semaphore()

    def greet(i, carry):
        @pl.when((i // 2 != y) | (i % 2 != k))
        def _():
            pl.semaphore_signal(barrier, inc=1, device_id=dev(z, i // 2, x, i % 2), device_id_type=MESH)

        @pl.when(i // 2 != x)
        def _():
            pl.semaphore_signal(barrier, inc=1, device_id=dev(z, y, i // 2, i % 2), device_id_type=MESH)

        return carry

    lax.fori_loop(0, 8, greet, 0)
    for step in range(1, PLANES):
        pl.semaphore_signal(barrier, inc=1, device_id=dev(lax.rem(z + step, 4), y, x, k), device_id_type=MESH)
    pl.semaphore_wait(barrier, 7 + 6 + 3)

    def planes(start):
        def one(c, carry):
            to = lax.rem(z - c + 4, 4)
            copy(
                start, src.at[pl.ds(pl.multiple_of(to * PIECE, PIECE), PIECE)],
                zbuf.at[pl.ds(pl.multiple_of(c * PIECE, PIECE), PIECE)], zs.at[c], zr.at[c], to, y, x, k,
            )
            return carry

        lax.fori_loop(0, PLANES, one, 0)

    def exchange(start, c):
        def one(i, carry):
            b, j = i // 2, i % 2
            piece = zbuf.at[pl.ds(pl.multiple_of(c * PIECE + i * SHARE, SHARE), SHARE)]
            in_row = pl.multiple_of(c * PIECE + (2 * y + k) * SHARE, SHARE)
            in_col = pl.multiple_of(c * PIECE + (2 * x + k) * SHARE, SHARE)
            copy(start, piece, erow.at[pl.ds(in_row, SHARE)], es.at[c, 0, i], er.at[c], z, b, x, j)
            copy(start, piece, ecol.at[pl.ds(in_col, SHARE)], es.at[c, 1, i], ec.at[c], z, y, b, j)
            return carry

        lax.fori_loop(0, 8, one, 0)

    def gather(start, c):
        at = pl.multiple_of(c * PIECE, PIECE)

        def one(i, carry):
            cx = lax.rem(x + 1 + i, 4)
            to = pl.multiple_of(c * CHUNK + x * PIECE, PIECE)
            full = (cx == y) | row_first(y, cx)

            @pl.when(full)
            def _():
                copy(start, erow.at[pl.ds(at, PIECE)], fbuf.at[pl.ds(to, PIECE)], gs.at[c, 0, i, 0], fr.at[c], z, y, cx, k)

            @pl.when(jnp.logical_not(full) & (k == 1))
            def _():
                for h in range(2):
                    copy(
                        start, erow.at[pl.ds(at + h * 64, 64)], hbuf.at[pl.ds(to + h * 64, 64)],
                        gs.at[c, 0, i, h], hr.at[c], z, y, cx, h,
                    )

            cy = lax.rem(y + 1 + i, 4)
            to_col = pl.multiple_of(c * CHUNK + y * PIECE, PIECE)

            @pl.when(cy == x)
            def _():
                copy(start, ecol.at[pl.ds(at, PIECE)], hbuf.at[pl.ds(to_col, PIECE)], gs.at[c, 1, i, 0], hr.at[c], z, cy, x, 1 - k)

            @pl.when((cy != x) & jnp.logical_not(row_first(cy, x)))
            def _():
                copy(start, ecol.at[pl.ds(at, PIECE)], fbuf.at[pl.ds(to_col, PIECE)], gs.at[c, 1, i, 0], fr.at[c], z, cy, x, k)

            @pl.when((cy != x) & row_first(cy, x) & (k == 0))
            def _():
                for h in range(2):
                    copy(
                        start, ecol.at[pl.ds(at + h * 64, 64)], hbuf.at[pl.ds(to_col + h * 64, 64)],
                        gs.at[c, 1, i, h], hr.at[c], z, cy, x, h,
                    )

            return carry

        lax.fori_loop(0, SIDE, one, 0)

    def sibling(start, c):
        def one(i, carry):
            half = hbuf.at[pl.ds(pl.multiple_of(c * CHUNK + i * PIECE + k * 64, 64), 64)]
            copy(start, half, half, ss.at[c, i], sr.at[c], z, y, x, 1 - k)
            return carry

        lax.fori_loop(0, SIDE, one, 0)

    def begin_exchange(c):
        arrive(zbuf.at[pl.ds(c * PIECE, PIECE)], zr.at[c])
        exchange(True, c)

    def begin_gather(c):
        arrive(erow.at[pl.ds(c * PIECE, PIECE)], er.at[c])
        arrive(ecol.at[pl.ds(c * PIECE, PIECE)], ec.at[c])
        gather(True, c)

    planes(True)
    begin_exchange(0)

    def feed(c, carry):
        begin_exchange(c + 1)
        begin_gather(c)
        return carry

    lax.fori_loop(0, PLANES - 1, feed, 0)
    begin_gather(PLANES - 1)

    first_slot = jnp.where(diagonal | by_row, 2 * y, 2 * x) + k
    other_slot = jnp.where(diagonal, 2 * y + 1 - k, jnp.where(by_row, 2 * x, 2 * y + 1))
    together = clus_ref[z * SLOTS + first_slot] == clus_ref[z * SLOTS + other_slot]

    def scores_of(left, i, right, j):
        a = left[pl.ds(pl.multiple_of(i * CHUNK, CHUNK), CHUNK), :]
        b = right[pl.ds(pl.multiple_of(j * CHUNK, CHUNK), CHUNK), :]
        return lax.dot_general(a, b, (((1,), (1,)), ((), ())), preferred_element_type=F32)

    def keep(scores, i, j, col, ok):
        over = scores[:, :128]
        for n in range(1, CHUNK // 128):
            over = jnp.maximum(over, scores[:, n * 128 : (n + 1) * 128])
        down = jnp.max(scores.reshape(CHUNK // 8, 8, CHUNK), axis=0)
        if ok is not None:
            over = jnp.where(ok, over, FLOOR)
            down = jnp.where(ok, down, FLOOR)
        at = pl.ds(pl.multiple_of(i * CHUNK, CHUNK), CHUNK)
        racc[at, :] = jnp.maximum(racc[at, :], over)
        col[j] = jnp.maximum(col[j], down)

    def compute(c, carry):
        here = pl.ds(pl.multiple_of(c * CHUNK, CHUNK), CHUNK)

        @pl.when(diagonal)
        def _():
            arrive(hbuf.at[here], hr.at[c])

        @pl.when(jnp.logical_not(diagonal))
        def _():
            arrive(hbuf.at[pl.ds(pl.multiple_of(c * CHUNK, 256), 256)], hr.at[c])
            sibling(True, c)

        arrive(fbuf.at[here], fr.at[c])

        @pl.when(diagonal)
        def _():
            def own(t, inner):
                keep(scores_of(fbuf, c, fbuf, t), c, t, fcacc, None)
                return inner

            lax.fori_loop(0, c, own, 0)
            scores = scores_of(fbuf, c, fbuf, c)
            same = lax.broadcasted_iota(I32, scores.shape, 0) == lax.broadcasted_iota(I32, scores.shape, 1)
            keep(jnp.where(same, FLOOR, scores), c, c, fcacc, None)

        @pl.when(jnp.logical_not(diagonal))
        def _():
            arrive(hbuf.at[pl.ds(pl.multiple_of(c * CHUNK, 256), 256)], sr.at[c])

        def cross(t, inner):
            i = jnp.where(t <= c, c, t - c - 1)
            j = jnp.where(t <= c, t, c)
            wanted = jnp.logical_not(diagonal) | ((k == 0) & (i < 2)) | ((k == 1) & (j >= 2))

            @pl.when(wanted)
            def _():
                keep(scores_of(fbuf, i, hbuf, j), i, j, cacc, together)

            return inner

        lax.fori_loop(0, 2 * c + 1, cross, 0)
        return carry

    lax.fori_loop(0, PLANES, compute, 0)

    for c in range(PLANES):
        down = jnp.max(cacc[c], axis=0, keepdims=True)
        own = jnp.max(fcacc[c], axis=0, keepdims=True)
        for s in range(SIDE):
            lanes = slice(s * 128, (s + 1) * 128)
            at = c * CHUNK + s * PIECE
            over = jnp.max(racc[at : at + PIECE, :].T, axis=0, keepdims=True)
            fsend[s, c : c + 1, :] = jnp.maximum(over, own[:, lanes])
            hsend[s, c : c + 1, :] = down[:, lanes]

    def results(start):
        def one(s, carry):
            to_row = diagonal | by_row

            @pl.when(to_row)
            def _():
                copy(start, fsend.at[s], rrow.at[x, 0], rs.at[0, s], rr.at[x, 0], z, y, s, k)

            @pl.when(jnp.logical_not(to_row))
            def _():
                copy(start, fsend.at[s], rcol.at[y, 0], rs.at[0, s], rc.at[y, 0], z, s, x, k)

            @pl.when(diagonal)
            def _():
                copy(start, hsend.at[s], rcol.at[y, 0], rs.at[1, s], rc.at[y, 0], z, s, x, 1 - k)

            @pl.when(jnp.logical_not(diagonal) & by_row)
            def _():
                copy(start, hsend.at[s], rcol.at[y, k], rs.at[1, s], rc.at[y, k], z, s, x, 0)

            @pl.when(jnp.logical_not(to_row))
            def _():
                copy(start, hsend.at[s], rrow.at[x, k], rs.at[1, s], rr.at[x, k], z, y, s, 1)

            return carry

        lax.fori_loop(0, SIDE, one, 0)

    results(True)

    def results_here(i, carry):
        full = (i == y) | row_first(y, i)

        @pl.when(full | (k == 1))
        def _():
            arrive(rrow.at[i, 0], rr.at[i, 0])

        @pl.when(jnp.logical_not(full) & (k == 1))
        def _():
            arrive(rrow.at[i, 1], rr.at[i, 1])

        part = (i != x) & row_first(i, x)

        @pl.when(jnp.logical_not(part) | (k == 0))
        def _():
            arrive(rcol.at[i, 0], rc.at[i, 0])

        @pl.when(part & (k == 0))
        def _():
            arrive(rcol.at[i, 1], rc.at[i, 1])

        return carry

    lax.fori_loop(0, SIDE, results_here, 0)
    for ref in (rrow, rcol):
        total = ref[0, 0]
        for i in range(SIDE):
            for j in range(2):
                if i or j:
                    total = jnp.maximum(total, ref[i, j])
        ref[0, 0] = total

    def unexchange(start):
        def one(i, carry):
            b, j = i // 2, i % 2
            copy(start, rrow.at[0, 0], brow.at[2 * y + k], bs.at[0, i], br.at[0], z, b, x, j)
            copy(start, rcol.at[0, 0], bcol.at[2 * x + k], bs.at[1, i], br.at[1], z, y, b, j)
            return carry

        lax.fori_loop(0, 8, one, 0)

    unexchange(True)
    arrive(brow, br.at[0])
    arrive(bcol, br.at[1])
    for c in range(PLANES):
        from_row = jnp.concatenate([brow[s, c : c + 1, :] for s in range(SLOTS)], axis=0)
        from_col = jnp.concatenate([bcol[s, c : c + 1, :] for s in range(SLOTS)], axis=0)
        from_row = pltpu.roll(from_row, lax.rem(128 - (2 * y + k) * SHARE, 128), 1)
        from_col = pltpu.roll(from_col, lax.rem(128 - (2 * x + k) * SHARE, 128), 1)
        zout[c] = jnp.maximum(from_row, from_col)

    def unplanes(start):
        def one(c, carry):
            copy(start, zout.at[c], fin.at[z], ts.at[c], tr.at[z], lax.rem(z + c, 4), y, x, k)
            return carry

        lax.fori_loop(0, PLANES, one, 0)

    unplanes(True)
    for p in range(PLANES):
        arrive(fin.at[p], tr.at[p])

    rows = PLANES * PIECE
    spread = jnp.broadcast_to(fin[...].reshape(PLANES * SLOTS, 1, 128), (PLANES * SLOTS, SHARE, 128)).reshape(rows, 128)
    lane = lax.broadcasted_iota(I32, (rows, 128), 1)
    sub = lax.rem(lax.broadcasted_iota(I32, (rows, 128), 0), SHARE)
    value = jnp.max(jnp.where(lane == sub, spread, FLOOR), axis=1, keepdims=True)
    pick = ids_ref[:, :1] == lax.broadcasted_iota(I32, (rows, rows), 1)
    out_ref[...] = jnp.max(jnp.where(pick, value, FLOOR), axis=0, keepdims=True)

    planes(False)

    def sent(c, carry):
        exchange(False, c)
        gather(False, c)

        @pl.when(jnp.logical_not(diagonal))
        def _():
            sibling(False, c)

        return carry

    lax.fori_loop(0, PLANES, sent, 0)
    results(False)
    unexchange(False)
    unplanes(False)


def by_planes(rows, ids, clus):
    vmem = pl.BlockSpec(memory_space=pltpu.VMEM)
    smem = pl.BlockSpec(memory_space=pltpu.SMEM)
    dma = pltpu.SemaphoreType.DMA
    best = pl.pallas_call(
        plane_kernel,
        out_shape=jax.ShapeDtypeStruct((1, rows.shape[0]), F32),
        in_specs=[smem, vmem, vmem],
        out_specs=vmem,
        scratch_shapes=[
            pltpu.VMEM((PLANES * PIECE, D), BF16),
            pltpu.VMEM((PLANES * PIECE, D), BF16),
            pltpu.VMEM((PLANES * PIECE, D), BF16),
            pltpu.VMEM((PLANES * CHUNK, D), BF16),
            pltpu.VMEM((PLANES * CHUNK, D), BF16),
            pltpu.VMEM((PLANES * CHUNK, 128), F32),
            pltpu.VMEM((PLANES, 8, CHUNK), F32),
            pltpu.VMEM((PLANES, 8, CHUNK), F32),
            pltpu.VMEM((SIDE, 8, 128), F32),
            pltpu.VMEM((SIDE, 8, 128), F32),
            pltpu.VMEM((SIDE, 2, 8, 128), F32),
            pltpu.VMEM((SIDE, 2, 8, 128), F32),
            pltpu.VMEM((SLOTS, 8, 128), F32),
            pltpu.VMEM((SLOTS, 8, 128), F32),
            pltpu.VMEM((PLANES, 8, 128), F32),
            pltpu.VMEM((PLANES, 8, 128), F32),
            dma((PLANES,)), dma((PLANES,)),
            dma((PLANES, 2, 8)), dma((PLANES,)), dma((PLANES,)),
            dma((PLANES, 2, SIDE, 2)), dma((PLANES,)), dma((PLANES,)),
            dma((PLANES, SIDE)), dma((PLANES,)),
            dma((2, SIDE)), dma((SIDE, 2)), dma((SIDE, 2)),
            dma((2, 8)), dma((2,)),
            dma((PLANES,)), dma((PLANES,)),
        ],
        compiler_params=pltpu.CompilerParams(
            collective_id=0, has_side_effects=True, vmem_limit_bytes=40 * 2**20
        ),
        name="by_planes",
    )(clus, rows, ids)
    return best.reshape(-1)


def shards(embeddings, member_rows, cluster_sizes, unit_pairs):
    rows, ids, clus, fits = prepare(embeddings, member_rows, cluster_sizes)
    return lax.cond(
        fits[0] > 0,
        lambda: by_planes(rows, ids, clus),
        lambda: direct(embeddings, member_rows, cluster_sizes, unit_pairs),
    )


def solution(mesh):
    placed = (P(AXES, None), P(), P(), P())
    return jax.shard_map(shards, mesh=mesh, in_specs=placed, out_specs=P(AXES), check_vma=False)
```

```python
import functools

import jax
import jax.numpy as jnp
from jax import lax
from jax.experimental import pallas as pl
from jax.experimental.pallas import tpu as pltpu
from jax.sharding import PartitionSpec as P

BLOCK = 256
GROUP_BLOCKS = 8
GROUP = BLOCK * GROUP_BLOCKS
AXES = ("store", "tile")
EPS = 1e-06
FLOOR = -4.0

MESH = pl.DeviceIdType.MESH
PLANES = 4
SIDE = 4
SLOTS = 8
SHARE = 16
PIECE = 8 * SHARE
CHUNK = SIDE * PIECE
HALF = PIECE // 2
D = 1024
BF16 = jnp.bfloat16
F32 = jnp.float32
I32 = jnp.int32


def compare_pair(left, right, same_group):
    span = 512

    def step(col_best, at):
        part = lax.dynamic_slice_in_dim(left, at, span)
        scores = lax.dot_general(part, right, (((1,), (1,)), ((), ())), preferred_element_type=F32)
        row_ids = at + lax.broadcasted_iota(I32, scores.shape, 0)
        col_ids = lax.broadcasted_iota(I32, scores.shape, 1)
        scores = jnp.where((row_ids == col_ids) & same_group, FLOOR, scores)
        return jnp.maximum(col_best, jnp.max(scores, axis=0)), jnp.max(scores, axis=1)

    first = jnp.full((right.shape[0],), FLOOR, F32)
    col_best, row_best = lax.scan(step, first, jnp.arange(0, left.shape[0], span, dtype=I32))
    return row_best.reshape(-1), col_best


def direct(embeddings, member_rows, cluster_sizes, unit_pairs):
    devices = lax.axis_size(AXES)
    me = lax.axis_index(AXES)
    rows_dev, width = embeddings.shape
    groups = member_rows.size // GROUP
    share = GROUP // devices
    owners = unit_pairs.shape[0]

    wide = embeddings.astype(F32)
    squares = jnp.sum(jnp.square(wide), axis=1, keepdims=True)
    unit = (wide * lax.rsqrt(squares + EPS)).astype(BF16)

    local = member_rows.reshape(-1, BLOCK) - me * rows_dev
    mine = (local >= 0) & (local < rows_dev)
    low = jnp.min(jnp.where(mine, local, rows_dev), axis=1)
    high = jnp.max(jnp.where(mine, local, -1), axis=1)
    order = jnp.stack([low, high], axis=1).reshape(rows_dev)
    pick = order[:, None] == jnp.arange(rows_dev, dtype=I32)[None, :]
    ordered = lax.dot_general(
        pick.astype(BF16), unit, (((1,), (0,)), ((), ())), preferred_element_type=F32
    ).astype(BF16)
    by_group = ordered.reshape(groups, share, width)

    first_group = (jnp.cumsum(cluster_sizes) - cluster_sizes) // GROUP
    pairs = unit_pairs[:, 0]
    usable = pairs[:, 0] >= 0
    sides = first_group[jnp.maximum(pairs[:, :1], 0)] + jnp.maximum(pairs[:, 1:], 0)
    outgoing = by_group[sides].reshape(owners, 2 * share, width)
    arrived = lax.all_to_all(outgoing, AXES, split_axis=0, concat_axis=0, tiled=True)
    arrived = arrived.reshape(devices, 2, share, width)
    left = arrived[:, 0].reshape(GROUP, width)
    right = arrived[:, 1].reshape(GROUP, width)
    row_best, col_best = compare_pair(left, right, sides[me, 0] == sides[me, 1])
    best = jnp.stack([row_best.reshape(devices, share), col_best.reshape(devices, share)], axis=1)
    best = jnp.where(usable[me], best, FLOOR).reshape(devices, 2 * share)
    back = lax.all_to_all(best, AXES, split_axis=0, concat_axis=0, tiled=True)
    back = back.reshape(owners * 2, share)
    of_group = sides.reshape(-1)[None, :] == jnp.arange(groups, dtype=I32)[:, None]
    best_slot = jnp.max(jnp.where(of_group[:, :, None], back[None], FLOOR), axis=1)
    return jnp.max(jnp.where(pick, best_slot.reshape(rows_dev, 1), FLOOR), axis=0)


def prepare_kernel(clusters, sizes_ref, emb_ref, members_ref, rows_ref, ids_ref, clus_ref, fits_ref, group_at, low_ref, high_ref, picked_ref):
    me = lax.axis_index("store") * (2 * SIDE * SIDE) + lax.axis_index("tile")
    rows_dev = emb_ref.shape[0]
    blocks = members_ref.shape[0] // 2
    local = [members_ref[pl.ds(h, blocks, stride=2), :] - me * rows_dev for h in range(2)]
    mine = [(part >= 0) & (part < rows_dev) for part in local]
    low = [jnp.where(ok, part, rows_dev) for ok, part in zip(mine, local)]
    high = [jnp.where(ok, part, -1) for ok, part in zip(mine, local)]
    low = jnp.min(jnp.minimum(*low), axis=1, keepdims=True)
    high = jnp.max(jnp.maximum(*high), axis=1, keepdims=True)
    low_ref[...] = jnp.broadcast_to(low, (blocks, 128))
    high_ref[...] = jnp.broadcast_to(high, (blocks, 128))
    wide = emb_ref[...].astype(F32)
    squares = jnp.sum(wide * wide, axis=1, keepdims=True)
    unit = (wide * lax.rsqrt(squares + EPS)).astype(BF16)
    column = lax.broadcasted_iota(I32, (blocks, rows_dev), 1)
    for h, wanted in enumerate((low, high)):
        pick = jnp.where(wanted == column, 1.0, 0.0).astype(BF16)
        picked_ref[h * blocks : (h + 1) * blocks, :] = lax.dot_general(
            pick, unit, (((1,), (0,)), ((), ())), preferred_element_type=F32
        )

    counts = [sizes_ref[c] // GROUP for c in range(clusters)]
    way = lax.broadcasted_iota(I32, (128, 128), 0) * 128 + lax.broadcasted_iota(I32, (128, 128), 1)
    loads = jnp.full((128, 128), counts[0], I32)
    for c in range(1, clusters):
        plane = lax.shift_right_logical(way, 2 * (c - 1)) & 3
        loads += lax.shift_left(jnp.full((128, 128), counts[c], I32), plane * 8)
    most = loads & 255
    for p in range(1, PLANES):
        most = jnp.maximum(most, lax.shift_right_logical(loads, 8 * p) & 255)
    chosen = jnp.min(most * 16384 + way)
    fits_ref[0] = (chosen // 16384 <= SLOTS).astype(I32)
    groups = PLANES * SLOTS
    for d in range(groups):
        group_at[d] = 0
        clus_ref[d] = -1
    used = [jnp.int32(0)] * PLANES
    start = jnp.int32(0)
    for c in range(clusters):
        plane = jnp.int32(0) if c == 0 else lax.shift_right_logical(chosen, 2 * (c - 1)) & 3
        offset = jnp.int32(0)
        for p in range(PLANES):
            offset = jnp.where(plane == p, used[p], offset)

        def put(i, carry, c=c, plane=plane, offset=offset, start=start):
            at = jnp.minimum(plane * SLOTS + offset + i, groups - 1)
            group_at[at] = jnp.minimum(start + i, groups - 1)
            clus_ref[at] = c
            return carry

        lax.fori_loop(0, counts[c], put, 0)
        for p in range(PLANES):
            used[p] = jnp.where(plane == p, used[p] + counts[c], used[p])
        start = start + counts[c]

    for d in range(groups):
        at = pl.multiple_of(group_at[d] * GROUP_BLOCKS, GROUP_BLOCKS)
        ids_ref[d * SHARE : d * SHARE + 8, :] = low_ref[pl.ds(at, 8), :]
        ids_ref[d * SHARE + 8 : d * SHARE + 16, :] = high_ref[pl.ds(at, 8), :]
        lower = picked_ref[pl.ds(at, 8), :]
        upper = picked_ref[pl.ds(pl.multiple_of(at + 256, 8), 8), :]
        rows_ref[d * SHARE : (d + 1) * SHARE, :] = jnp.concatenate([lower, upper], axis=0).astype(BF16)


def prepare(embeddings, member_rows, cluster_sizes):
    rows_dev, width = embeddings.shape
    vmem = pl.BlockSpec(memory_space=pltpu.VMEM)
    smem = pl.BlockSpec(memory_space=pltpu.SMEM)
    groups = PLANES * SLOTS
    return pl.pallas_call(
        functools.partial(prepare_kernel, cluster_sizes.shape[0]),
        out_shape=(
            jax.ShapeDtypeStruct((rows_dev, width), BF16),
            jax.ShapeDtypeStruct((rows_dev, 128), I32),
            jax.ShapeDtypeStruct((groups,), I32),
            jax.ShapeDtypeStruct((1,), I32),
        ),
        in_specs=[smem, vmem, vmem],
        out_specs=(vmem, vmem, smem, smem),
        scratch_shapes=[
            pltpu.SMEM((groups,), I32),
            pltpu.VMEM((member_rows.size // BLOCK, 128), I32),
            pltpu.VMEM((member_rows.size // BLOCK, 128), I32),
            pltpu.VMEM((rows_dev, width), F32),
        ],
        compiler_params=pltpu.CompilerParams(vmem_limit_bytes=32 * 2**20),
        name="prepare",
    )(cluster_sizes, embeddings, member_rows.reshape(-1, BLOCK // 2))


def plane_kernel(
    clus_ref, src, ids_ref, out_ref,
    zbuf, erow, ecol, fbuf, hbuf, racc, cacc, fcacc, fsend, hsend,
    rrow, rcol, brow, bcol, zout, fin,
    zs, zr, es, er, ec, gs, vs, fr, hr, ss, sr,
    rs, rr, bs, br, ts,
):
    z = lax.axis_index("store")
    tile = lax.axis_index("tile")
    y, x, k = tile // 8, (tile // 2) % 4, tile % 2

    def far(from_, to, ssem, rsem, dz, dy, dx, dk):
        pltpu.make_async_remote_copy(
            from_, to, ssem, rsem, device_id=(dz, dy * 8 + dx * 2 + dk), device_id_type=MESH
        ).start()

    def near(from_, to, rsem):
        pltpu.make_async_copy(from_, to, rsem).start()

    def arrive(ref, sem):
        pltpu.make_async_copy(ref, ref, sem).wait()

    def row_first(cy, cx):
        step = (cx - cy) & 3
        return (step == 1) | ((step == 2) & (cy < 2))

    diagonal = y == x
    across = jnp.logical_not(diagonal)
    by_row = row_first(y, x)
    in_row, in_col = 2 * y + k, 2 * x + k

    for ref in (rrow, rcol):
        ref[...] = jnp.full(ref.shape, FLOOR, F32)

    barrier = pltpu.get_barrier_semaphore()

    def greet(dz, dy, dx, dk):
        pl.semaphore_signal(barrier, inc=1, device_id=(dz, dy * 8 + dx * 2 + dk), device_id_type=MESH)

    for n in range(1, 8):
        i = (in_row + n) & 7
        greet(z, i // 2, x, i & 1)
    for n in range(1, SIDE):
        for core in range(2):
            greet(z, y, (x + n) & 3, core)
        greet((z + n) & 3, y, x, k)
    pl.semaphore_wait(barrier, 7 + 6 + 3)

    def hop(c):
        return (0, 1, 3, 2)[c]

    def chunk(c):
        return pl.ds(c * PIECE if isinstance(c, int) else pl.multiple_of(c * PIECE, PIECE), PIECE)

    def exchange(c):
        arrive(zbuf.at[chunk(c)], zr.at[c])
        row_at = pl.ds(pl.multiple_of(c * PIECE + in_row * SHARE, SHARE), SHARE)
        col_at = pl.ds(pl.multiple_of(c * PIECE + in_col * SHARE, SHARE), SHARE)

        def piece(i):
            return zbuf.at[pl.ds(pl.multiple_of(c * PIECE + i * SHARE, SHARE), SHARE)]

        for n in range(1, 8):
            i = (in_row + n) & 7
            far(piece(i), erow.at[row_at], es, er.at[c], z, i // 2, x, i & 1)
            i = (in_col + n) & 7
            far(piece(i), ecol.at[col_at], es, ec.at[c], z, y, i // 2, i & 1)
        near(piece(in_row), erow.at[row_at], er.at[c])
        near(piece(in_col), ecol.at[col_at], ec.at[c])

    lines = []
    for role, (ebuf, esem, line, pos) in enumerate(((erow, er, y, x), (ecol, ec, x, y))):
        mine = (pos - line) & 3
        special = k == role
        wide = line < 2
        goals = []
        for n in (1, 3, 0):
            r = (mine + n) & 3
            p = (pos + n) & 3
            whole = (r == 1) | ((r == 2) & wide) | ((r == 0) & special)
            halves = ((r == 3) | ((r == 2) & jnp.logical_not(wide))) & jnp.logical_not(special)
            goals.append((n, p, whole, halves))
        lines.append((role, ebuf, esem, pos, goals))

    def gather(c):
        for role, ebuf, esem, pos, goals in lines:
            arrive(ebuf.at[chunk(c)], esem.at[c])
            to = c * SIDE + pos
            for n, p, whole, halves in goals:
                py, px = (y, p) if role == 0 else (p, x)

                def send_whole(role=role, ebuf=ebuf, n=n, py=py, px=px, to=to):
                    if n:
                        far(ebuf.at[chunk(c)], fbuf.at[to], gs.at[role, n, 0], fr.at[c, 0], z, py, px, k)
                    else:
                        near(ebuf.at[chunk(c)], fbuf.at[to], fr.at[c, 0])

                def send_halves(role=role, ebuf=ebuf, n=n, py=py, px=px, to=to):
                    if n:
                        for h in range(2):
                            part = pl.ds(h * HALF, HALF)
                            far(
                                ebuf.at[pl.ds(c * PIECE + h * HALF, HALF)], hbuf.at[to, part],
                                gs.at[role, n, h], hr.at[c, 0], z, py, px, h,
                            )
                    else:
                        for h, go in ((k, None), (1 - k, 1 - k)):
                            part = pl.ds(pl.multiple_of(h * HALF, HALF), HALF)
                            here = ebuf.at[pl.ds(pl.multiple_of(c * PIECE + h * HALF, HALF), HALF)]
                            if go is None:
                                near(here, hbuf.at[to, part], hr.at[c, 0])
                            else:
                                far(here, hbuf.at[to, part], gs.at[role, 0, 0], hr.at[c, 0], z, y, x, go)

                pl.when(whole)(send_whole)
                pl.when(halves)(send_halves)

    def gather_sent():
        for role, _, _, _, goals in lines:
            for n, _, whole, halves in goals:

                def sent_whole(role=role, n=n):
                    if n:
                        arrive(fbuf.at[pl.ds(0, PLANES)], gs.at[role, n, 0])

                def sent_halves(role=role, n=n):
                    for h in range(2 if n else 1):
                        arrive(fbuf.at[pl.ds(0, PLANES), pl.ds(0, HALF)], gs.at[role, n, h])

                if n:
                    pl.when(whole)(sent_whole)
                pl.when(halves)(sent_halves)

    f_row = jnp.where(diagonal, k == 0, by_row)
    f_line, f_pos = jnp.where(f_row, y, x), jnp.where(f_row, x, y)
    h_line, h_pos = f_pos, f_line
    f_rel, h_rel = (f_pos - f_line) & 3, (h_pos - h_line) & 3
    f_special = k == jnp.where(f_row, 0, 1)
    h_core = jnp.where(f_row, 0, 1)
    my_half = pl.ds(pl.multiple_of(k * HALF, HALF), HALF)

    def relay(c):
        def f_to(r):
            p = (f_line + r) & 3
            return jnp.where(f_row, y, p), jnp.where(f_row, p, x)

        def h_to(r):
            p = (h_line + r) & 3
            return jnp.where(f_row, p, y), jnp.where(f_row, x, p)

        def whole(s, r, sem):
            if c is None:
                return arrive(fbuf.at[pl.ds(0, PLANES)], vs.at[sem])
            part = fbuf.at[c * SIDE + ((f_line + s) & 3)]
            far(part, part, vs.at[sem], fr.at[c, 1], z, *f_to(r), k)

        def half(s, r, sem, into, arrived, core):
            if c is None:
                return arrive(fbuf.at[pl.ds(0, PLANES), pl.ds(0, HALF)], vs.at[sem])
            at = c * SIDE + ((h_line + s) & 3)
            far(hbuf.at[at, my_half], into.at[at, my_half], vs.at[sem], arrived.at[c, 1], z, *h_to(r), core)

        @pl.when(f_rel == 0)
        def _():
            whole(3, 1, 0)

        @pl.when((f_rel == 1) & f_special)
        def _():
            whole(2, 0, 0)

            @pl.when(f_line < 2)
            def _():
                whole(0, 2, 1)

        @pl.when((f_rel == 2) & jnp.logical_not(f_special))
        def _():
            whole(3, 1, 0)
            for h in range(2):
                if c is None:
                    arrive(fbuf.at[pl.ds(0, PLANES), pl.ds(0, HALF)], vs.at[1 + h])
                else:
                    at, part = c * SIDE + ((f_line + 1) & 3), pl.ds(h * HALF, HALF)
                    far(fbuf.at[at, part], hbuf.at[at, part], vs.at[1 + h], hr.at[c, 1], z, *f_to(3), h)

        @pl.when(across & (h_rel == 2))
        def _():
            half(3, 1, 3, fbuf, fr, h_core)
            half(1, 3, 4, hbuf, hr, k)

        @pl.when(across & (h_rel == 3))
        def _():
            @pl.when(h_line < 2)
            def _():
                half(0, 2, 3, fbuf, fr, h_core)

            @pl.when(h_line >= 2)
            def _():
                half(0, 2, 3, hbuf, hr, k)

    def pass_on(c):
        arrive(fbuf.at[pl.ds(0, 3)], fr.at[c, 0])

        @pl.when(across)
        def _():
            arrive(fbuf.at[pl.ds(0, 3), pl.ds(0, HALF)], hr.at[c, 0])

        relay(c)

    def settle(c):
        arrive(fbuf.at[0], fr.at[c, 1])
        part = pl.ds(c * SIDE, SIDE)

        @pl.when(diagonal)
        def _():
            far(fbuf.at[part], hbuf.at[part], ss, sr.at[c], z, y, x, 1 - k)
            arrive(hbuf.at[part], sr.at[c])

        @pl.when(across)
        def _():
            arrive(fbuf.at[0, pl.ds(0, HALF)], hr.at[c, 1])
            far(hbuf.at[part, my_half], hbuf.at[part, my_half], ss, sr.at[c], z, y, x, 1 - k)
            arrive(fbuf.at[pl.ds(0, SIDE), pl.ds(0, HALF)], sr.at[c])

    for c in range(1, PLANES):
        to = (z - hop(c)) & 3
        far(src.at[chunk(to)], zbuf.at[chunk(c)], zs, zr.at[c], to, y, x, k)
    near(src.at[chunk(z)], zbuf.at[chunk(0)], zr.at[0])
    exchange(0)
    gather(0)
    for ref in (racc, cacc, fcacc, fsend, hsend):
        ref[...] = jnp.full(ref.shape, FLOOR, F32)
    exchange(1)
    exchange(2)
    exchange(3)
    gather(1)
    pass_on(0)
    gather(2)
    pass_on(1)
    gather(3)

    first_slot = jnp.where(f_row, 2 * y, 2 * x) + k
    other_slot = jnp.where(diagonal, 2 * y + 1 - k, jnp.where(by_row, 2 * x, 2 * y + 1))
    together = clus_ref[z * SLOTS + first_slot] == clus_ref[z * SLOTS + other_slot]

    def scores_of(left, i, right, j):
        a = left[pl.ds(i * SIDE, SIDE)].reshape(CHUNK, D)
        b = right[pl.ds(j * SIDE, SIDE)].reshape(CHUNK, D)
        return lax.dot_general(a, b, (((1,), (1,)), ((), ())), preferred_element_type=F32)

    def keep(scores, i, j, col, ok):
        over = scores[:, :128]
        for n in range(1, CHUNK // 128):
            over = jnp.maximum(over, scores[:, n * 128 : (n + 1) * 128])
        down = jnp.max(scores.reshape(CHUNK // 8, 8, CHUNK), axis=0)
        if ok is not None:
            over = jnp.where(ok, over, FLOOR)
            down = jnp.where(ok, down, FLOOR)
        at = pl.ds(i * CHUNK if isinstance(i, int) else pl.multiple_of(i * CHUNK, CHUNK), CHUNK)
        racc[at, :] = jnp.maximum(racc[at, :], over)
        col[j] = jnp.maximum(col[j], down)

    def compute(c):
        @pl.when(diagonal)
        def _():
            def own(t, inner):
                keep(scores_of(fbuf, c, fbuf, t), c, t, fcacc, None)
                return inner

            lax.fori_loop(0, c, own, 0)
            scores = scores_of(fbuf, c, fbuf, c)
            same = lax.broadcasted_iota(I32, scores.shape, 0) == lax.broadcasted_iota(I32, scores.shape, 1)
            keep(jnp.where(same, FLOOR, scores), c, c, fcacc, None)

        def cross(t, inner):
            i = jnp.where(t <= c, c, t - c - 1)
            j = jnp.where(t <= c, t, c)
            wanted = across | ((k == 0) & (i < 2)) | ((k == 1) & (j >= 2))

            @pl.when(wanted)
            def _():
                keep(scores_of(fbuf, i, hbuf, j), i, j, cacc, together)

            return inner

        lax.fori_loop(0, 2 * c + 1, cross, 0)

    def work(c, carry):
        @pl.when(c == 2)
        def _():
            arrive(fbuf.at[pl.ds(0, 3)], zs)
            arrive(fbuf.at[pl.ds(0, 7)], es)
            gather_sent()

        settle(c)
        compute(c)

        @pl.when(c + 2 < PLANES)
        def _():
            pass_on(c + 2)

        return carry

    lax.fori_loop(0, PLANES, work, 0)

    for c in range(PLANES):
        down = jnp.max(cacc[c], axis=0, keepdims=True)
        own = jnp.max(fcacc[c], axis=0, keepdims=True)
        for s in range(SIDE):
            lanes = slice(s * 128, (s + 1) * 128)
            at = c * CHUNK + s * PIECE
            over = jnp.max(racc[at : at + PIECE, :].T, axis=0, keepdims=True)
            fsend[s, c : c + 1, :] = jnp.maximum(over, own[:, lanes])
            hsend[s, c : c + 1, :] = down[:, lanes]

    second = jnp.where(diagonal, 1, k)

    @pl.when(f_row)
    def _():
        core = jnp.where(diagonal, 1, 0)
        for n in range(1, SIDE):
            s, t = (x + n) & 3, (y + n) & 3
            far(fsend.at[s], rrow.at[2 * x], rs, rr.at[0], z, y, s, k)
            far(hsend.at[t], rcol.at[2 * y + second], rs, rr.at[1], z, t, x, core)
        near(fsend.at[x], rrow.at[2 * x], rr.at[0])

        @pl.when(core == k)
        def _():
            near(hsend.at[y], rcol.at[2 * y + second], rr.at[1])

        @pl.when(core != k)
        def _():
            far(hsend.at[y], rcol.at[2 * y + second], ts, rr.at[1], z, y, x, core)

    @pl.when(jnp.logical_not(f_row))
    def _():
        core = jnp.where(diagonal, 0, 1)
        for n in range(1, SIDE):
            s, t = (y + n) & 3, (x + n) & 3
            far(fsend.at[s], rcol.at[2 * y], rs, rr.at[1], z, s, x, k)
            far(hsend.at[t], rrow.at[2 * x + second], rs, rr.at[0], z, y, t, core)
        near(fsend.at[y], rcol.at[2 * y], rr.at[1])

        @pl.when(core == k)
        def _():
            near(hsend.at[x], rrow.at[2 * x + second], rr.at[0])

        @pl.when(core != k)
        def _():
            far(hsend.at[x], rrow.at[2 * x + second], ts, rr.at[0], z, y, x, core)

    for role, (ref, line) in enumerate(((rrow, y), (rcol, x))):
        count = jnp.where(line < 2, 4, jnp.where(k == role, 3, 5))
        for n in (3, 4, 5):

            @pl.when(count == n)
            def _(ref=ref, role=role, n=n):
                arrive(ref.at[pl.ds(0, n)], rr.at[role])

        total = ref[0]
        for i in range(1, 2 * SIDE):
            total = jnp.maximum(total, ref[i])
        ref[0] = total

    for n in range(1, 8):
        i = (in_row + n) & 7
        far(rrow.at[0], brow.at[in_row], bs, br.at[0], z, i // 2, x, i & 1)
        i = (in_col + n) & 7
        far(rcol.at[0], bcol.at[in_col], bs, br.at[1], z, y, i // 2, i & 1)
    near(rrow.at[0], brow.at[in_row], br.at[0])
    near(rcol.at[0], bcol.at[in_col], br.at[1])
    arrive(brow, br.at[0])
    arrive(bcol, br.at[1])
    for c in range(PLANES):
        from_row = jnp.concatenate([brow[s, c : c + 1, :] for s in range(SLOTS)], axis=0)
        from_col = jnp.concatenate([bcol[s, c : c + 1, :] for s in range(SLOTS)], axis=0)
        from_row = pltpu.roll(from_row, (128 - in_row * SHARE) & 127, 1)
        from_col = pltpu.roll(from_col, (128 - in_col * SHARE) & 127, 1)
        value = jnp.maximum(from_row, from_col)
        if c:
            zout[c] = value
            far(zout.at[c], fin.at[c], bs, br.at[2], (z + hop(c)) & 3, y, x, k)
        else:
            fin[0] = value
    arrive(fin.at[pl.ds(1, 3)], br.at[2])

    rows = PLANES * PIECE
    lane = lax.broadcasted_iota(I32, (PIECE, 128), 1)
    sub = lax.broadcasted_iota(I32, (PIECE, 128), 0) & (SHARE - 1)
    best = jnp.full((1, rows), FLOOR, F32)
    for c in range(PLANES):
        spread = jnp.broadcast_to(fin[c].reshape(SLOTS, 1, 128), (SLOTS, SHARE, 128)).reshape(PIECE, 128)
        value = jnp.max(jnp.where(lane == sub, spread, FLOOR), axis=1, keepdims=True)
        pick = ids_ref[chunk((z - hop(c)) & 3), :][:, :1] == lax.broadcasted_iota(I32, (PIECE, rows), 1)
        best = jnp.maximum(best, jnp.max(jnp.where(pick, value, FLOOR), axis=0, keepdims=True))
    out_ref[...] = best

    relay(None)

    @pl.when(diagonal)
    def _():
        arrive(fbuf, ss)

    @pl.when(across)
    def _():
        arrive(fbuf.at[pl.ds(0, 4 * PLANES), pl.ds(0, HALF)], ss)

    arrive(brow.at[pl.ds(0, 6)], rs)

    @pl.when(jnp.where(diagonal, True, k != jnp.where(f_row, 0, 1)))
    def _():
        arrive(brow.at[0], ts)

    arrive(racc.at[pl.ds(0, 17 * 8)], bs)


def by_planes(rows, ids, clus):
    vmem = pl.BlockSpec(memory_space=pltpu.VMEM)
    smem = pl.BlockSpec(memory_space=pltpu.SMEM)
    dma = pltpu.SemaphoreType.DMA
    best = pl.pallas_call(
        plane_kernel,
        out_shape=jax.ShapeDtypeStruct((1, rows.shape[0]), F32),
        in_specs=[smem, vmem, vmem],
        out_specs=vmem,
        scratch_shapes=[
            pltpu.VMEM((PLANES * PIECE, D), BF16),
            pltpu.VMEM((PLANES * PIECE, D), BF16),
            pltpu.VMEM((PLANES * PIECE, D), BF16),
            pltpu.VMEM((PLANES * SIDE, PIECE, D), BF16),
            pltpu.VMEM((PLANES * SIDE, PIECE, D), BF16),
            pltpu.VMEM((PLANES * CHUNK, 128), F32),
            pltpu.VMEM((PLANES, 8, CHUNK), F32),
            pltpu.VMEM((PLANES, 8, CHUNK), F32),
            pltpu.VMEM((SIDE, 8, 128), F32),
            pltpu.VMEM((SIDE, 8, 128), F32),
            pltpu.VMEM((SIDE * 2, 8, 128), F32),
            pltpu.VMEM((SIDE * 2, 8, 128), F32),
            pltpu.VMEM((SLOTS, 8, 128), F32),
            pltpu.VMEM((SLOTS, 8, 128), F32),
            pltpu.VMEM((PLANES, 8, 128), F32),
            pltpu.VMEM((PLANES, 8, 128), F32),
            dma, dma((PLANES,)),
            dma, dma((PLANES,)), dma((PLANES,)),
            dma((2, SIDE, 2)), dma((5,)), dma((PLANES, 2)), dma((PLANES, 2)),
            dma, dma((PLANES,)),
            dma, dma((2,)),
            dma, dma((3,)),
            dma,
        ],
        compiler_params=pltpu.CompilerParams(
            collective_id=0, has_side_effects=True, vmem_limit_bytes=40 * 2**20
        ),
        name="by_planes",
    )(clus, rows, ids)
    return best.reshape(-1)


def shards(embeddings, member_rows, cluster_sizes, unit_pairs):
    rows, ids, clus, fits = prepare(embeddings, member_rows, cluster_sizes)
    return lax.cond(
        fits[0] > 0,
        lambda: by_planes(rows, ids, clus),
        lambda: direct(embeddings, member_rows, cluster_sizes, unit_pairs),
    )


def solution(mesh):
    placed = (P(AXES, None), P(), P(), P())
    return jax.shard_map(shards, mesh=mesh, in_specs=placed, out_specs=P(AXES), check_vma=False)
```

```python
import functools

import jax
import jax.numpy as jnp
from jax import lax
from jax.experimental import pallas as pl
from jax.experimental.pallas import tpu as pltpu
from jax.sharding import PartitionSpec as P

BLOCK = 256
GROUP_BLOCKS = 8
GROUP = BLOCK * GROUP_BLOCKS
AXES = ("store", "tile")
EPS = 1e-06
FLOOR = -4.0

MESH = pl.DeviceIdType.MESH
PLANES = 4
SIDE = 4
SLOTS = 8
SHARE = 16
PIECE = 8 * SHARE
CHUNK = SIDE * PIECE
HALF = PIECE // 2
D = 1024
BF16 = jnp.bfloat16
F32 = jnp.float32
I32 = jnp.int32


def compare_pair(left, right, same_group):
    span = 512

    def step(col_best, at):
        part = lax.dynamic_slice_in_dim(left, at, span)
        scores = lax.dot_general(part, right, (((1,), (1,)), ((), ())), preferred_element_type=F32)
        row_ids = at + lax.broadcasted_iota(I32, scores.shape, 0)
        col_ids = lax.broadcasted_iota(I32, scores.shape, 1)
        scores = jnp.where((row_ids == col_ids) & same_group, FLOOR, scores)
        return jnp.maximum(col_best, jnp.max(scores, axis=0)), jnp.max(scores, axis=1)

    first = jnp.full((right.shape[0],), FLOOR, F32)
    col_best, row_best = lax.scan(step, first, jnp.arange(0, left.shape[0], span, dtype=I32))
    return row_best.reshape(-1), col_best


def direct(embeddings, member_rows, cluster_sizes, unit_pairs):
    devices = lax.axis_size(AXES)
    me = lax.axis_index(AXES)
    rows_dev, width = embeddings.shape
    groups = member_rows.size // GROUP
    share = GROUP // devices
    owners = unit_pairs.shape[0]

    wide = embeddings.astype(F32)
    squares = jnp.sum(jnp.square(wide), axis=1, keepdims=True)
    unit = (wide * lax.rsqrt(squares + EPS)).astype(BF16)

    local = member_rows.reshape(-1, BLOCK) - me * rows_dev
    mine = (local >= 0) & (local < rows_dev)
    low = jnp.min(jnp.where(mine, local, rows_dev), axis=1)
    high = jnp.max(jnp.where(mine, local, -1), axis=1)
    order = jnp.stack([low, high], axis=1).reshape(rows_dev)
    pick = order[:, None] == jnp.arange(rows_dev, dtype=I32)[None, :]
    ordered = lax.dot_general(
        pick.astype(BF16), unit, (((1,), (0,)), ((), ())), preferred_element_type=F32
    ).astype(BF16)
    by_group = ordered.reshape(groups, share, width)

    first_group = (jnp.cumsum(cluster_sizes) - cluster_sizes) // GROUP
    pairs = unit_pairs[:, 0]
    usable = pairs[:, 0] >= 0
    sides = first_group[jnp.maximum(pairs[:, :1], 0)] + jnp.maximum(pairs[:, 1:], 0)
    outgoing = by_group[sides].reshape(owners, 2 * share, width)
    arrived = lax.all_to_all(outgoing, AXES, split_axis=0, concat_axis=0, tiled=True)
    arrived = arrived.reshape(devices, 2, share, width)
    left = arrived[:, 0].reshape(GROUP, width)
    right = arrived[:, 1].reshape(GROUP, width)
    row_best, col_best = compare_pair(left, right, sides[me, 0] == sides[me, 1])
    best = jnp.stack([row_best.reshape(devices, share), col_best.reshape(devices, share)], axis=1)
    best = jnp.where(usable[me], best, FLOOR).reshape(devices, 2 * share)
    back = lax.all_to_all(best, AXES, split_axis=0, concat_axis=0, tiled=True)
    back = back.reshape(owners * 2, share)
    of_group = sides.reshape(-1)[None, :] == jnp.arange(groups, dtype=I32)[:, None]
    best_slot = jnp.max(jnp.where(of_group[:, :, None], back[None], FLOOR), axis=1)
    return jnp.max(jnp.where(pick, best_slot.reshape(rows_dev, 1), FLOOR), axis=0)


def prepare_kernel(clusters, sizes_ref, emb_ref, members_ref, rows_ref, ids_ref, clus_ref, fits_ref, group_at, low_ref, high_ref, picked_ref):
    me = lax.axis_index("store") * (2 * SIDE * SIDE) + lax.axis_index("tile")
    rows_dev = emb_ref.shape[0]
    blocks = members_ref.shape[0] // 2
    local = [members_ref[pl.ds(h, blocks, stride=2), :] - me * rows_dev for h in range(2)]
    mine = [(part >= 0) & (part < rows_dev) for part in local]
    low = [jnp.where(ok, part, rows_dev) for ok, part in zip(mine, local)]
    high = [jnp.where(ok, part, -1) for ok, part in zip(mine, local)]
    low = jnp.min(jnp.minimum(*low), axis=1, keepdims=True)
    high = jnp.max(jnp.maximum(*high), axis=1, keepdims=True)
    low_ref[...] = jnp.broadcast_to(low, (blocks, 128))
    high_ref[...] = jnp.broadcast_to(high, (blocks, 128))
    wide = emb_ref[...].astype(F32)
    squares = jnp.sum(wide * wide, axis=1, keepdims=True)
    unit = (wide * lax.rsqrt(squares + EPS)).astype(BF16)
    column = lax.broadcasted_iota(I32, (blocks, rows_dev), 1)
    for h, wanted in enumerate((low, high)):
        pick = jnp.where(wanted == column, 1.0, 0.0).astype(BF16)
        picked_ref[h * blocks : (h + 1) * blocks, :] = lax.dot_general(
            pick, unit, (((1,), (0,)), ((), ())), preferred_element_type=F32
        )

    counts = [sizes_ref[c] // GROUP for c in range(clusters)]
    way = lax.broadcasted_iota(I32, (128, 128), 0) * 128 + lax.broadcasted_iota(I32, (128, 128), 1)
    loads = jnp.full((128, 128), counts[0], I32)
    for c in range(1, clusters):
        plane = lax.shift_right_logical(way, 2 * (c - 1)) & 3
        loads += lax.shift_left(jnp.full((128, 128), counts[c], I32), plane * 8)
    most = loads & 255
    for p in range(1, PLANES):
        most = jnp.maximum(most, lax.shift_right_logical(loads, 8 * p) & 255)
    chosen = jnp.min(most * 16384 + way)
    fits_ref[0] = (chosen // 16384 <= SLOTS).astype(I32)
    groups = PLANES * SLOTS
    for d in range(groups):
        group_at[d] = 0
        clus_ref[d] = -1
    used = [jnp.int32(0)] * PLANES
    start = jnp.int32(0)
    for c in range(clusters):
        plane = jnp.int32(0) if c == 0 else lax.shift_right_logical(chosen, 2 * (c - 1)) & 3
        offset = jnp.int32(0)
        for p in range(PLANES):
            offset = jnp.where(plane == p, used[p], offset)

        def put(i, carry, c=c, plane=plane, offset=offset, start=start):
            at = jnp.minimum(plane * SLOTS + offset + i, groups - 1)
            group_at[at] = jnp.minimum(start + i, groups - 1)
            clus_ref[at] = c
            return carry

        lax.fori_loop(0, counts[c], put, 0)
        for p in range(PLANES):
            used[p] = jnp.where(plane == p, used[p] + counts[c], used[p])
        start = start + counts[c]

    for d in range(groups):
        at = pl.multiple_of(group_at[d] * GROUP_BLOCKS, GROUP_BLOCKS)
        ids_ref[d * SHARE : d * SHARE + 8, :] = low_ref[pl.ds(at, 8), :]
        ids_ref[d * SHARE + 8 : d * SHARE + 16, :] = high_ref[pl.ds(at, 8), :]
        lower = picked_ref[pl.ds(at, 8), :]
        upper = picked_ref[pl.ds(pl.multiple_of(at + 256, 8), 8), :]
        rows_ref[d * SHARE : (d + 1) * SHARE, :] = jnp.concatenate([lower, upper], axis=0).astype(BF16)


def prepare(embeddings, member_rows, cluster_sizes):
    rows_dev, width = embeddings.shape
    vmem = pl.BlockSpec(memory_space=pltpu.VMEM)
    smem = pl.BlockSpec(memory_space=pltpu.SMEM)
    groups = PLANES * SLOTS
    return pl.pallas_call(
        functools.partial(prepare_kernel, cluster_sizes.shape[0]),
        out_shape=(
            jax.ShapeDtypeStruct((rows_dev, width), BF16),
            jax.ShapeDtypeStruct((rows_dev, 128), I32),
            jax.ShapeDtypeStruct((groups,), I32),
            jax.ShapeDtypeStruct((1,), I32),
        ),
        in_specs=[smem, vmem, vmem],
        out_specs=(vmem, vmem, smem, smem),
        scratch_shapes=[
            pltpu.SMEM((groups,), I32),
            pltpu.VMEM((member_rows.size // BLOCK, 128), I32),
            pltpu.VMEM((member_rows.size // BLOCK, 128), I32),
            pltpu.VMEM((rows_dev, width), F32),
        ],
        compiler_params=pltpu.CompilerParams(vmem_limit_bytes=32 * 2**20),
        name="prepare",
    )(cluster_sizes, embeddings, member_rows.reshape(-1, BLOCK // 2))


def plane_kernel(
    clus_ref, src, ids_ref, out_ref,
    zbuf, erow, ecol, fbuf, hbuf, racc, cacc, fcacc, fsend, hsend,
    rrow, rcol, brow, bcol, zout, fin,
    zs, zr, es, er, ec, gs, vs, fr, hr,
    rs, rr, bs, br, ts,
):
    z = lax.axis_index("store")
    tile = lax.axis_index("tile")
    y, x, k = tile // 8, (tile // 2) % 4, tile % 2

    def far(from_, to, ssem, rsem, dz, dy, dx, dk):
        pltpu.make_async_remote_copy(
            from_, to, ssem, rsem, device_id=(dz, dy * 8 + dx * 2 + dk), device_id_type=MESH
        ).start()

    def near(from_, to, rsem):
        pltpu.make_async_copy(from_, to, rsem).start()

    def arrive(ref, sem):
        pltpu.make_async_copy(ref, ref, sem).wait()

    diagonal = y == x
    in_row, in_col = 2 * y + k, 2 * x + k

    barrier = pltpu.get_barrier_semaphore()

    def greet(dz, dy, dx, dk):
        pl.semaphore_signal(barrier, inc=1, device_id=(dz, dy * 8 + dx * 2 + dk), device_id_type=MESH)

    for n in range(1, 8):
        i = (in_row + n) & 7
        greet(z, i // 2, x, i & 1)
    for n in range(1, SIDE):
        for core in range(2):
            greet(z, y, (x + n) & 3, core)
        greet((z + n) & 3, y, x, k)
    pl.semaphore_wait(barrier, 7 + 6 + 3)

    def hop(c):
        return (0, 1, 3, 2)[c]

    def chunk(c):
        return pl.ds(c * PIECE if isinstance(c, int) else pl.multiple_of(c * PIECE, PIECE), PIECE)

    def exchange(c):
        if c:
            arrive(zbuf.at[chunk(c)], zr.at[c])
        row_at = pl.ds(pl.multiple_of(c * PIECE + in_row * SHARE, SHARE), SHARE)
        col_at = pl.ds(pl.multiple_of(c * PIECE + in_col * SHARE, SHARE), SHARE)

        def piece(i):
            if c:
                return zbuf.at[pl.ds(pl.multiple_of(c * PIECE + i * SHARE, SHARE), SHARE)]
            return src.at[pl.ds(pl.multiple_of(z * PIECE + i * SHARE, SHARE), SHARE)]

        for n in range(1, 8):
            i = (in_row + n) & 7
            far(piece(i), erow.at[row_at], es, er.at[c], z, i // 2, x, i & 1)
            i = (in_col + n) & 7
            far(piece(i), ecol.at[col_at], es, ec.at[c], z, y, i // 2, i & 1)
        near(piece(in_row), erow.at[row_at], er.at[c])
        near(piece(in_col), ecol.at[col_at], ec.at[c])

    def col_core(cy, member):
        return jnp.where(cy < x, member, 1 - member)

    member = col_core(y, k)

    def gather(c):
        arrive(erow.at[chunk(c)], er.at[c])
        arrive(ecol.at[chunk(c)], ec.at[c])
        mine, at_row, at_col = chunk(c), c * SIDE + x, c * SIDE + y
        for way, n in enumerate((1, 3)):
            px, py = (x + n) & 3, (y + n) & 3
            far(erow.at[mine], fbuf.at[at_row], gs.at[0], fr.at[c, way], z, y, px, k)
            far(ecol.at[mine], hbuf.at[at_col], gs.at[0], hr.at[c, way], z, py, x, col_core(py, k))
        near(erow.at[mine], fbuf.at[at_row], fr.at[c, 2])

        @pl.when(y < x)
        def _():
            near(ecol.at[mine], hbuf.at[at_col], hr.at[c, 2])

        @pl.when(y >= x)
        def _():
            far(ecol.at[mine], hbuf.at[at_col], gs.at[1], hr.at[c, 2], z, y, x, 1 - k)

    def pass_on(c):
        for way, n in enumerate((1, 3)):
            part = pl.ds(way * HALF, HALF)
            px, py = (x + n) & 3, (y + n) & 3
            at = c * SIDE + ((x - n) & 3)
            arrive(fbuf.at[at], fr.at[c, way])
            far(fbuf.at[at, part], fbuf.at[at, part], vs, fr.at[c, 3], z, y, px, k)
            at = c * SIDE + ((y - n) & 3)
            arrive(hbuf.at[at], hr.at[c, way])
            far(hbuf.at[at, part], hbuf.at[at, part], vs, hr.at[c, 3], z, py, x, col_core(py, member))

    def settle(c):
        for sem in (2, 3):
            arrive(fbuf.at[0], fr.at[c, sem])
            arrive(hbuf.at[0], hr.at[c, sem])

    for c in range(1, PLANES):
        to = (z - hop(c)) & 3
        far(src.at[chunk(to)], zbuf.at[chunk(c)], zs, zr.at[c], to, y, x, k)
    exchange(0)
    gather(0)
    for ref in (racc, cacc, fcacc, fsend, hsend):
        ref[...] = jnp.full(ref.shape, FLOOR, F32)
    exchange(1)
    exchange(2)
    exchange(3)
    gather(1)
    pass_on(0)
    gather(2)
    pass_on(1)
    gather(3)

    first_slot = 2 * y + k
    other_slot = 2 * x + member
    together = clus_ref[z * SLOTS + first_slot] == clus_ref[z * SLOTS + other_slot]

    def scores_of(left, i, right, j):
        a = left[pl.ds(i * SIDE, SIDE)].reshape(CHUNK, D)
        b = right[pl.ds(j * SIDE, SIDE)].reshape(CHUNK, D)
        return lax.dot_general(a, b, (((1,), (1,)), ((), ())), preferred_element_type=F32)

    def keep(scores, i, j, col, ok):
        over = scores[:, :128]
        for n in range(1, CHUNK // 128):
            over = jnp.maximum(over, scores[:, n * 128 : (n + 1) * 128])
        down = jnp.max(scores.reshape(CHUNK // 8, 8, CHUNK), axis=0)
        if ok is not None:
            over = jnp.where(ok, over, FLOOR)
            down = jnp.where(ok, down, FLOOR)
        at = pl.ds(i * CHUNK if isinstance(i, int) else pl.multiple_of(i * CHUNK, CHUNK), CHUNK)
        racc[at, :] = jnp.maximum(racc[at, :], over)
        col[j] = jnp.maximum(col[j], down)

    def compute(c):
        @pl.when(diagonal)
        def _():
            def own(t, inner):
                keep(scores_of(fbuf, c, fbuf, t), c, t, fcacc, None)
                return inner

            lax.fori_loop(0, c, own, 0)
            scores = scores_of(fbuf, c, fbuf, c)
            same = lax.broadcasted_iota(I32, scores.shape, 0) == lax.broadcasted_iota(I32, scores.shape, 1)
            keep(jnp.where(same, FLOOR, scores), c, c, fcacc, None)

        def cross(t, inner):
            i = jnp.where(t <= c, c, t - c - 1)
            j = jnp.where(t <= c, t, c)
            wanted = jnp.logical_not(diagonal) | (i < j) | ((i == j) & ((k == 0) == (i < 2)))

            @pl.when(wanted)
            def _():
                keep(scores_of(fbuf, i, hbuf, j), i, j, cacc, together)

            return inner

        lax.fori_loop(0, 2 * c + 1, cross, 0)

    def work(c, carry):
        @pl.when(c == 2)
        def _():
            arrive(fbuf.at[pl.ds(0, 3)], zs)
            arrive(fbuf.at[pl.ds(0, 7)], es)
            arrive(fbuf, gs.at[0])

        settle(c)
        compute(c)

        @pl.when(c + 2 < PLANES)
        def _():
            pass_on(c + 2)

        return carry

    lax.fori_loop(0, PLANES, work, 0)

    for c in range(PLANES):
        down = jnp.max(cacc[c], axis=0, keepdims=True)
        own = jnp.max(fcacc[c], axis=0, keepdims=True)
        for s in range(SIDE):
            lanes = slice(s * 128, (s + 1) * 128)
            at = c * CHUNK + s * PIECE
            over = jnp.max(racc[at : at + PIECE, :].T, axis=0, keepdims=True)
            fsend[s, c : c + 1, :] = jnp.maximum(over, own[:, lanes])
            hsend[s, c : c + 1, :] = down[:, lanes]

    for n in range(1, SIDE):
        s, t = (x + n) & 3, (y + n) & 3
        far(fsend.at[s], rrow.at[x], rs, rr.at[0], z, y, s, k)
        far(hsend.at[t], rcol.at[y], rs, rr.at[1], z, t, x, member)
    near(fsend.at[x], rrow.at[x], rr.at[0])

    @pl.when(y < x)
    def _():
        near(hsend.at[y], rcol.at[y], rr.at[1])

    @pl.when(y >= x)
    def _():
        far(hsend.at[y], rcol.at[y], ts, rr.at[1], z, y, x, 1 - k)

    for role, ref in enumerate((rrow, rcol)):
        arrive(ref, rr.at[role])
        total = ref[0]
        for i in range(1, SIDE):
            total = jnp.maximum(total, ref[i])
        ref[0] = total

    for n in range(1, 8):
        i = (in_row + n) & 7
        far(rrow.at[0], brow.at[in_row], bs, br.at[0], z, i // 2, x, i & 1)
        i = (in_col + n) & 7
        far(rcol.at[0], bcol.at[in_col], bs, br.at[1], z, y, i // 2, i & 1)
    near(rrow.at[0], brow.at[in_row], br.at[0])
    near(rcol.at[0], bcol.at[in_col], br.at[1])
    arrive(brow, br.at[0])
    arrive(bcol, br.at[1])
    for c in range(PLANES):
        from_row = jnp.concatenate([brow[s, c : c + 1, :] for s in range(SLOTS)], axis=0)
        from_col = jnp.concatenate([bcol[s, c : c + 1, :] for s in range(SLOTS)], axis=0)
        from_row = pltpu.roll(from_row, (128 - in_row * SHARE) & 127, 1)
        from_col = pltpu.roll(from_col, (128 - in_col * SHARE) & 127, 1)
        value = jnp.maximum(from_row, from_col)
        if c:
            zout[c] = value
            far(zout.at[c], fin.at[c], bs, br.at[2], (z + hop(c)) & 3, y, x, k)
        else:
            fin[0] = value
    arrive(fin.at[pl.ds(1, 3)], br.at[2])

    rows = PLANES * PIECE
    lane = lax.broadcasted_iota(I32, (PIECE, 128), 1)
    sub = lax.broadcasted_iota(I32, (PIECE, 128), 0) & (SHARE - 1)
    best = jnp.full((1, rows), FLOOR, F32)
    for c in range(PLANES):
        spread = jnp.broadcast_to(fin[c].reshape(SLOTS, 1, 128), (SLOTS, SHARE, 128)).reshape(PIECE, 128)
        value = jnp.max(jnp.where(lane == sub, spread, FLOOR), axis=1, keepdims=True)
        pick = ids_ref[chunk((z - hop(c)) & 3), :][:, :1] == lax.broadcasted_iota(I32, (PIECE, rows), 1)
        best = jnp.maximum(best, jnp.max(jnp.where(pick, value, FLOOR), axis=0, keepdims=True))
    out_ref[...] = best

    arrive(fbuf.at[pl.ds(0, 8)], vs)
    arrive(brow.at[pl.ds(0, 6)], rs)

    @pl.when(y >= x)
    def _():
        arrive(fbuf.at[pl.ds(0, PLANES)], gs.at[1])
        arrive(brow.at[0], ts)

    arrive(racc.at[pl.ds(0, 17 * 8)], bs)


def by_planes(rows, ids, clus):
    vmem = pl.BlockSpec(memory_space=pltpu.VMEM)
    smem = pl.BlockSpec(memory_space=pltpu.SMEM)
    dma = pltpu.SemaphoreType.DMA
    best = pl.pallas_call(
        plane_kernel,
        out_shape=jax.ShapeDtypeStruct((1, rows.shape[0]), F32),
        in_specs=[smem, vmem, vmem],
        out_specs=vmem,
        scratch_shapes=[
            pltpu.VMEM((PLANES * PIECE, D), BF16),
            pltpu.VMEM((PLANES * PIECE, D), BF16),
            pltpu.VMEM((PLANES * PIECE, D), BF16),
            pltpu.VMEM((PLANES * SIDE, PIECE, D), BF16),
            pltpu.VMEM((PLANES * SIDE, PIECE, D), BF16),
            pltpu.VMEM((PLANES * CHUNK, 128), F32),
            pltpu.VMEM((PLANES, 8, CHUNK), F32),
            pltpu.VMEM((PLANES, 8, CHUNK), F32),
            pltpu.VMEM((SIDE, 8, 128), F32),
            pltpu.VMEM((SIDE, 8, 128), F32),
            pltpu.VMEM((SIDE, 8, 128), F32),
            pltpu.VMEM((SIDE, 8, 128), F32),
            pltpu.VMEM((SLOTS, 8, 128), F32),
            pltpu.VMEM((SLOTS, 8, 128), F32),
            pltpu.VMEM((PLANES, 8, 128), F32),
            pltpu.VMEM((PLANES, 8, 128), F32),
            dma, dma((PLANES,)),
            dma, dma((PLANES,)), dma((PLANES,)),
            dma((2,)), dma, dma((PLANES, 4)), dma((PLANES, 4)),
            dma, dma((2,)),
            dma, dma((3,)),
            dma,
        ],
        compiler_params=pltpu.CompilerParams(
            collective_id=0, has_side_effects=True, vmem_limit_bytes=40 * 2**20
        ),
        name="by_planes",
    )(clus, rows, ids)
    return best.reshape(-1)


def shards(embeddings, member_rows, cluster_sizes, unit_pairs):
    rows, ids, clus, fits = prepare(embeddings, member_rows, cluster_sizes)
    return lax.cond(
        fits[0] > 0,
        lambda: by_planes(rows, ids, clus),
        lambda: direct(embeddings, member_rows, cluster_sizes, unit_pairs),
    )


def solution(mesh):
    placed = (P(AXES, None), P(), P(), P())
    return jax.shard_map(shards, mesh=mesh, in_specs=placed, out_specs=P(AXES), check_vma=False)
```

```python
import functools

import jax
import jax.numpy as jnp
from jax import lax
from jax.experimental import pallas as pl
from jax.experimental.pallas import tpu as pltpu
from jax.sharding import PartitionSpec as P

BLOCK = 256
GROUP_BLOCKS = 8
GROUP = BLOCK * GROUP_BLOCKS
AXES = ("store", "tile")
EPS = 1e-06
FLOOR = -4.0

MESH = pl.DeviceIdType.MESH
PLANES = 4
SIDE = 4
SLOTS = 8
SHARE = 16
PIECE = 8 * SHARE
CHUNK = SIDE * PIECE
HALF = PIECE // 2
D = 1024
BF16 = jnp.bfloat16
F32 = jnp.float32
I32 = jnp.int32


def compare_pair(left, right, same_group):
    span = 512

    def step(col_best, at):
        part = lax.dynamic_slice_in_dim(left, at, span)
        scores = lax.dot_general(part, right, (((1,), (1,)), ((), ())), preferred_element_type=F32)
        row_ids = at + lax.broadcasted_iota(I32, scores.shape, 0)
        col_ids = lax.broadcasted_iota(I32, scores.shape, 1)
        scores = jnp.where((row_ids == col_ids) & same_group, FLOOR, scores)
        return jnp.maximum(col_best, jnp.max(scores, axis=0)), jnp.max(scores, axis=1)

    first = jnp.full((right.shape[0],), FLOOR, F32)
    col_best, row_best = lax.scan(step, first, jnp.arange(0, left.shape[0], span, dtype=I32))
    return row_best.reshape(-1), col_best


def direct(embeddings, member_rows, cluster_sizes, unit_pairs):
    devices = lax.axis_size(AXES)
    me = lax.axis_index(AXES)
    rows_dev, width = embeddings.shape
    groups = member_rows.size // GROUP
    share = GROUP // devices
    owners = unit_pairs.shape[0]

    wide = embeddings.astype(F32)
    squares = jnp.sum(jnp.square(wide), axis=1, keepdims=True)
    unit = (wide * lax.rsqrt(squares + EPS)).astype(BF16)

    local = member_rows.reshape(-1, BLOCK) - me * rows_dev
    mine = (local >= 0) & (local < rows_dev)
    low = jnp.min(jnp.where(mine, local, rows_dev), axis=1)
    high = jnp.max(jnp.where(mine, local, -1), axis=1)
    order = jnp.stack([low, high], axis=1).reshape(rows_dev)
    pick = order[:, None] == jnp.arange(rows_dev, dtype=I32)[None, :]
    ordered = lax.dot_general(
        pick.astype(BF16), unit, (((1,), (0,)), ((), ())), preferred_element_type=F32
    ).astype(BF16)
    by_group = ordered.reshape(groups, share, width)

    first_group = (jnp.cumsum(cluster_sizes) - cluster_sizes) // GROUP
    pairs = unit_pairs[:, 0]
    usable = pairs[:, 0] >= 0
    sides = first_group[jnp.maximum(pairs[:, :1], 0)] + jnp.maximum(pairs[:, 1:], 0)
    outgoing = by_group[sides].reshape(owners, 2 * share, width)
    arrived = lax.all_to_all(outgoing, AXES, split_axis=0, concat_axis=0, tiled=True)
    arrived = arrived.reshape(devices, 2, share, width)
    left = arrived[:, 0].reshape(GROUP, width)
    right = arrived[:, 1].reshape(GROUP, width)
    row_best, col_best = compare_pair(left, right, sides[me, 0] == sides[me, 1])
    best = jnp.stack([row_best.reshape(devices, share), col_best.reshape(devices, share)], axis=1)
    best = jnp.where(usable[me], best, FLOOR).reshape(devices, 2 * share)
    back = lax.all_to_all(best, AXES, split_axis=0, concat_axis=0, tiled=True)
    back = back.reshape(owners * 2, share)
    of_group = sides.reshape(-1)[None, :] == jnp.arange(groups, dtype=I32)[:, None]
    best_slot = jnp.max(jnp.where(of_group[:, :, None], back[None], FLOOR), axis=1)
    return jnp.max(jnp.where(pick, best_slot.reshape(rows_dev, 1), FLOOR), axis=0)


def prepare_kernel(clusters, sizes_ref, emb_ref, members_ref, rows_ref, ids_ref, clus_ref, fits_ref, group_at, low_ref, high_ref, picked_ref):
    me = lax.axis_index("store") * (2 * SIDE * SIDE) + lax.axis_index("tile")
    rows_dev = emb_ref.shape[0]
    blocks = members_ref.shape[0] // 2
    local = [members_ref[pl.ds(h, blocks, stride=2), :] - me * rows_dev for h in range(2)]
    mine = [(part >= 0) & (part < rows_dev) for part in local]
    low = [jnp.where(ok, part, rows_dev) for ok, part in zip(mine, local)]
    high = [jnp.where(ok, part, -1) for ok, part in zip(mine, local)]
    low = jnp.min(jnp.minimum(*low), axis=1, keepdims=True)
    high = jnp.max(jnp.maximum(*high), axis=1, keepdims=True)
    low_ref[...] = jnp.broadcast_to(low, (blocks, 128))
    high_ref[...] = jnp.broadcast_to(high, (blocks, 128))
    wide = emb_ref[...].astype(F32)
    squares = jnp.sum(wide * wide, axis=1, keepdims=True)
    unit = (wide * lax.rsqrt(squares + EPS)).astype(BF16)
    column = lax.broadcasted_iota(I32, (blocks, rows_dev), 1)
    for h, wanted in enumerate((low, high)):
        pick = jnp.where(wanted == column, 1.0, 0.0).astype(BF16)
        picked_ref[h * blocks : (h + 1) * blocks, :] = lax.dot_general(
            pick, unit, (((1,), (0,)), ((), ())), preferred_element_type=F32
        )

    counts = [sizes_ref[c] // GROUP for c in range(clusters)]
    way = lax.broadcasted_iota(I32, (128, 128), 0) * 128 + lax.broadcasted_iota(I32, (128, 128), 1)
    loads = jnp.full((128, 128), counts[0], I32)
    for c in range(1, clusters):
        plane = lax.shift_right_logical(way, 2 * (c - 1)) & 3
        loads += lax.shift_left(jnp.full((128, 128), counts[c], I32), plane * 8)
    most = loads & 255
    for p in range(1, PLANES):
        most = jnp.maximum(most, lax.shift_right_logical(loads, 8 * p) & 255)
    chosen = jnp.min(most * 16384 + way)
    fits_ref[0] = (chosen // 16384 <= SLOTS).astype(I32)
    groups = PLANES * SLOTS
    for d in range(groups):
        group_at[d] = 0
        clus_ref[d] = -1
    used = [jnp.int32(0)] * PLANES
    start = jnp.int32(0)
    for c in range(clusters):
        plane = jnp.int32(0) if c == 0 else lax.shift_right_logical(chosen, 2 * (c - 1)) & 3
        offset = jnp.int32(0)
        for p in range(PLANES):
            offset = jnp.where(plane == p, used[p], offset)

        def put(i, carry, c=c, plane=plane, offset=offset, start=start):
            at = jnp.minimum(plane * SLOTS + offset + i, groups - 1)
            group_at[at] = jnp.minimum(start + i, groups - 1)
            clus_ref[at] = c
            return carry

        lax.fori_loop(0, counts[c], put, 0)
        for p in range(PLANES):
            used[p] = jnp.where(plane == p, used[p] + counts[c], used[p])
        start = start + counts[c]

    for d in range(groups):
        at = pl.multiple_of(group_at[d] * GROUP_BLOCKS, GROUP_BLOCKS)
        ids_ref[d * SHARE : d * SHARE + 8, :] = low_ref[pl.ds(at, 8), :]
        ids_ref[d * SHARE + 8 : d * SHARE + 16, :] = high_ref[pl.ds(at, 8), :]
        lower = picked_ref[pl.ds(at, 8), :]
        upper = picked_ref[pl.ds(pl.multiple_of(at + 256, 8), 8), :]
        rows_ref[d * SHARE : (d + 1) * SHARE, :] = jnp.concatenate([lower, upper], axis=0).astype(BF16)


def prepare(embeddings, member_rows, cluster_sizes):
    rows_dev, width = embeddings.shape
    vmem = pl.BlockSpec(memory_space=pltpu.VMEM)
    smem = pl.BlockSpec(memory_space=pltpu.SMEM)
    groups = PLANES * SLOTS
    return pl.pallas_call(
        functools.partial(prepare_kernel, cluster_sizes.shape[0]),
        out_shape=(
            jax.ShapeDtypeStruct((rows_dev, width), BF16),
            jax.ShapeDtypeStruct((rows_dev, 128), I32),
            jax.ShapeDtypeStruct((groups,), I32),
            jax.ShapeDtypeStruct((1,), I32),
        ),
        in_specs=[smem, vmem, vmem],
        out_specs=(vmem, vmem, smem, smem),
        scratch_shapes=[
            pltpu.SMEM((groups,), I32),
            pltpu.VMEM((member_rows.size // BLOCK, 128), I32),
            pltpu.VMEM((member_rows.size // BLOCK, 128), I32),
            pltpu.VMEM((rows_dev, width), F32),
        ],
        compiler_params=pltpu.CompilerParams(vmem_limit_bytes=32 * 2**20),
        name="prepare",
    )(cluster_sizes, embeddings, member_rows.reshape(-1, BLOCK // 2))


def plane_kernel(
    clus_ref, src, ids_hbm, out_ref,
    ids_ref, zbuf, erow, ecol, fbuf, hbuf, racc, hacc, cacc, fcacc, fsend, hsend,
    rrow, rcol, brow, bcol, zout, fin,
    zs, zr, es, er, ec, gs, vs, fr, hr,
    rs, rr, bs, br, ts, ids_sem,
):
    z = lax.axis_index("store")
    tile = lax.axis_index("tile")
    y, x, k = tile // 8, (tile // 2) % 4, tile % 2

    def far(from_, to, ssem, rsem, dz, dy, dx, dk):
        pltpu.make_async_remote_copy(
            from_, to, ssem, rsem, device_id=(dz, dy * 8 + dx * 2 + dk), device_id_type=MESH
        ).start()

    def near(from_, to, rsem):
        pltpu.make_async_copy(from_, to, rsem).start()

    def arrive(ref, sem):
        pltpu.make_async_copy(ref, ref, sem).wait()

    diagonal = y == x
    in_row, in_col = 2 * y + k, 2 * x + k

    barrier = pltpu.get_barrier_semaphore()

    def greet(dz, dy, dx, dk):
        pl.semaphore_signal(barrier, inc=1, device_id=(dz, dy * 8 + dx * 2 + dk), device_id_type=MESH)

    for n in range(1, 8):
        i = (in_row + n) & 7
        greet(z, i // 2, x, i & 1)
    for n in range(1, SIDE):
        for core in range(2):
            greet(z, y, (x + n) & 3, core)
        greet((z + n) & 3, y, x, k)
    pl.semaphore_wait(barrier, 7 + 6 + 3)

    def hop(c):
        return (0, 1, 3, 2)[c]

    def chunk(c):
        return pl.ds(c * PIECE if isinstance(c, int) else pl.multiple_of(c * PIECE, PIECE), PIECE)

    def exchange(c):
        if c:
            arrive(zbuf.at[chunk(c)], zr.at[c])
        row_at = pl.ds(pl.multiple_of(c * PIECE + in_row * SHARE, SHARE), SHARE)
        col_at = pl.ds(pl.multiple_of(c * PIECE + in_col * SHARE, SHARE), SHARE)

        def piece(i):
            if c:
                return zbuf.at[pl.ds(pl.multiple_of(c * PIECE + i * SHARE, SHARE), SHARE)]
            return src.at[pl.ds(pl.multiple_of(z * PIECE + i * SHARE, SHARE), SHARE)]

        for n in range(1, 8):
            i = (in_row + n) & 7
            far(piece(i), erow.at[row_at], es, er.at[c], z, i // 2, x, i & 1)
            i = (in_col + n) & 7
            far(piece(i), ecol.at[col_at], es, ec.at[c], z, y, i // 2, i & 1)
        near(piece(in_row), erow.at[row_at], er.at[c])
        near(piece(in_col), ecol.at[col_at], ec.at[c])

    def col_core(cy, member):
        return jnp.where(cy < x, member, 1 - member)

    member = col_core(y, k)

    def gather(c):
        arrive(erow.at[chunk(c)], er.at[c])
        arrive(ecol.at[chunk(c)], ec.at[c])
        mine, at = chunk(c), c * SIDE
        for way, n in enumerate((1, 3)):
            px, py = (x + n) & 3, (y + n) & 3
            far(erow.at[mine], fbuf.at[at + 1 + way], gs.at[0], fr.at[c, way], z, y, px, k)
            far(ecol.at[mine], hbuf.at[at + 1 + way], gs.at[0], hr.at[c, way], z, py, x, col_core(py, k))
        near(erow.at[mine], fbuf.at[at], fr.at[c, 2])

        @pl.when(y < x)
        def _():
            near(ecol.at[mine], hbuf.at[at], hr.at[c, 2])

        @pl.when(y >= x)
        def _():
            far(ecol.at[mine], hbuf.at[at], gs.at[1], hr.at[c, 2], z, y, x, 1 - k)

    def pass_on(c):
        for way, n in enumerate((1, 3)):
            part = pl.ds(way * HALF, HALF)
            px, py = (x + n) & 3, (y + n) & 3
            at, to = c * SIDE + 1 + way, c * SIDE + 3
            arrive(fbuf.at[at], fr.at[c, way])
            far(fbuf.at[at, part], fbuf.at[to, part], vs, fr.at[c, 3], z, y, px, k)
            arrive(hbuf.at[at], hr.at[c, way])
            far(hbuf.at[at, part], hbuf.at[to, part], vs, hr.at[c, 3], z, py, x, col_core(py, member))

    def settle(c, shares=(2, 3)):
        for sem in shares:
            arrive(fbuf.at[0], fr.at[c, sem])
            arrive(hbuf.at[0], hr.at[c, sem])

    for c in range(1, PLANES):
        to = (z - hop(c)) & 3
        far(src.at[chunk(to)], zbuf.at[chunk(c)], zs, zr.at[c], to, y, x, k)
    exchange(0)
    near(ids_hbm, ids_ref, ids_sem)
    gather(0)
    for ref in (racc, hacc, cacc, fcacc, fsend, hsend):
        ref[...] = jnp.full(ref.shape, FLOOR, F32)
    exchange(1)
    exchange(2)
    exchange(3)
    gather(1)
    pass_on(0)
    gather(2)
    pass_on(1)
    pass_on(2)
    gather(3)

    first_slot = 2 * y + k
    other_slot = 2 * x + member
    together = clus_ref[z * SLOTS + first_slot] == clus_ref[z * SLOTS + other_slot]

    def meet(left, i, rows, right, j, cols, col, ok=None, same=False, rowmax=None):
        a = left[pl.ds(i, rows)].reshape(rows * PIECE, D)
        b = right[pl.ds(j, cols)].reshape(cols * PIECE, D)
        scores = lax.dot_general(a, b, (((1,), (1,)), ((), ())), preferred_element_type=F32)
        if same:
            eye = lax.broadcasted_iota(I32, scores.shape, 0) == lax.broadcasted_iota(I32, scores.shape, 1)
            scores = jnp.where(eye, FLOOR, scores)
        over = scores[:, :PIECE]
        for n in range(1, cols):
            over = jnp.maximum(over, scores[:, n * PIECE : (n + 1) * PIECE])
        down = jnp.max(scores.reshape(rows * PIECE // 8, 8, cols * PIECE), axis=0)
        if ok is not None:
            over = jnp.where(ok, over, FLOOR)
            down = jnp.where(ok, down, FLOOR)
        at = pl.ds(i * PIECE if isinstance(i, int) else pl.multiple_of(i * PIECE, PIECE), rows * PIECE)
        if rowmax is None:
            racc[at, :] = jnp.maximum(racc[at, :], over)
        else:
            rowmax[...] = jnp.maximum(rowmax[...], over)
        for n in range(cols):
            col[j + n] = jnp.maximum(col[j + n], down[:, n * PIECE : (n + 1) * PIECE])

    off = jnp.logical_not(diagonal)

    def corner(i, rows, t):
        @pl.when(diagonal)
        def _():
            meet(fbuf, i, rows, fbuf, t * SIDE, SIDE, fcacc)

        @pl.when(off)
        def _():
            meet(fbuf, i, rows, hbuf, t * SIDE, SIDE, cacc, together)

        meet(fbuf, t * SIDE, SIDE, hbuf, i, rows, cacc, together)

    def middle(i, rows, takes):
        @pl.when(diagonal)
        def _():
            meet(fbuf, i, rows, fbuf, i, rows, fcacc, same=True)

        @pl.when(off | takes)
        def _():
            meet(fbuf, i, rows, hbuf, i, rows, cacc, together)

    def compute(c):
        def before(t, carry):
            corner(c * SIDE, SIDE, t)
            return carry

        lax.fori_loop(0, c, before, 0)
        middle(c * SIDE, SIDE, (k == 0) == (c < 2))

    def early(c, carry):
        settle(c)
        compute(c)
        return carry

    lax.fori_loop(0, 3, early, 0)
    pass_on(3)
    arrive(fbuf.at[pl.ds(0, 3)], zs)
    arrive(fbuf.at[pl.ds(0, 7)], es)
    arrive(fbuf, gs.at[0])

    last, takes = 3 * SIDE, k == 1
    settle(3, (2,))

    def ahead(t, carry):
        corner(last, 3, t)
        return carry

    lax.fori_loop(0, 3, ahead, 0)
    middle(last, 3, takes)
    def flat(s, c):
        at = (c * SIDE + s) * PIECE
        fsend[s, c : c + 1, :] = jnp.max(racc[at : at + PIECE, :].T, axis=0, keepdims=True)

    for s in range(SIDE):
        for c in range(PLANES):
            if (s, c) != (3, 3):
                flat(s, c)
    settle(3, (3,))

    @pl.when(off)
    def _():
        meet(fbuf, 15, 1, hbuf, 0, 16, cacc, together)
        meet(hbuf, 15, 1, fbuf, 0, 15, fcacc, together, rowmax=hacc)

    @pl.when(diagonal)
    def _():
        meet(fbuf, 15, 1, fbuf, 0, 15, fcacc)
        meet(fbuf, 15, 1, fbuf, 15, 1, fcacc, same=True)
        meet(hbuf, 15, 1, fbuf, 0, 12, fcacc, together, rowmax=hacc)

    @pl.when(diagonal & takes)
    def _():
        meet(fbuf, 15, 1, hbuf, 12, 4, cacc, together)
        meet(hbuf, 15, 1, fbuf, 12, 3, fcacc, together, rowmax=hacc)

    places = (0, 3, 1, 2)
    for s in (1, 2, 3, 0):
        for c in range(PLANES):
            best = jnp.max(cacc[c * SIDE + s], axis=0, keepdims=True)
            if (s, c) == (3, 3):
                best = jnp.maximum(best, jnp.max(hacc[...].T, axis=0, keepdims=True))
            hsend[s, c : c + 1, :] = best
        if s:
            far(hsend.at[s], rcol.at[y], rs, rr.at[1], z, (y + places[s]) & 3, x, member)

    @pl.when(y < x)
    def _():
        near(hsend.at[0], rcol.at[y], rr.at[1])

    @pl.when(y >= x)
    def _():
        far(hsend.at[0], rcol.at[y], ts, rr.at[1], z, y, x, 1 - k)

    flat(3, 3)
    for s in (1, 2, 3, 0):
        for c in range(PLANES):
            best = jnp.max(fcacc[c * SIDE + s], axis=0, keepdims=True)
            fsend[s, c : c + 1, :] = jnp.maximum(fsend[s, c : c + 1, :], best)
        if s:
            far(fsend.at[s], rrow.at[x], rs, rr.at[0], z, y, (x + places[s]) & 3, k)
        else:
            near(fsend.at[0], rrow.at[x], rr.at[0])

    def total(ref, sem):
        arrive(ref, sem)
        best = ref[0]
        for i in range(1, SIDE):
            best = jnp.maximum(best, ref[i])
        ref[0] = best

    total(rcol, rr.at[1])
    for n in range(1, 8):
        i = (in_col + n) & 7
        far(rcol.at[0], bcol.at[in_col], bs, br.at[1], z, y, i // 2, i & 1)
    near(rcol.at[0], bcol.at[in_col], br.at[1])
    total(rrow, rr.at[0])
    for n in range(1, 8):
        i = (in_row + n) & 7
        far(rrow.at[0], brow.at[in_row], bs, br.at[0], z, i // 2, x, i & 1)
    near(rrow.at[0], brow.at[in_row], br.at[0])
    arrive(brow, br.at[0])
    arrive(bcol, br.at[1])
    for c in range(PLANES):
        from_row = jnp.concatenate([brow[s, c : c + 1, :] for s in range(SLOTS)], axis=0)
        from_col = jnp.concatenate([bcol[s, c : c + 1, :] for s in range(SLOTS)], axis=0)
        from_row = pltpu.roll(from_row, (128 - in_row * SHARE) & 127, 1)
        from_col = pltpu.roll(from_col, (128 - in_col * SHARE) & 127, 1)
        value = jnp.maximum(from_row, from_col)
        if c:
            zout[c] = value
            far(zout.at[c], fin.at[c], bs, br.at[2], (z + hop(c)) & 3, y, x, k)
        else:
            fin[0] = value
    arrive(fin.at[pl.ds(1, 3)], br.at[2])

    arrive(ids_ref, ids_sem)
    rows = PLANES * PIECE
    lane = lax.broadcasted_iota(I32, (PIECE, 128), 1)
    sub = lax.broadcasted_iota(I32, (PIECE, 128), 0) & (SHARE - 1)
    best = jnp.full((1, rows), FLOOR, F32)
    for c in range(PLANES):
        spread = jnp.broadcast_to(fin[c].reshape(SLOTS, 1, 128), (SLOTS, SHARE, 128)).reshape(PIECE, 128)
        value = jnp.max(jnp.where(lane == sub, spread, FLOOR), axis=1, keepdims=True)
        pick = ids_ref[chunk((z - hop(c)) & 3), :][:, :1] == lax.broadcasted_iota(I32, (PIECE, rows), 1)
        best = jnp.maximum(best, jnp.max(jnp.where(pick, value, FLOOR), axis=0, keepdims=True))
    out_ref[...] = best

    arrive(fbuf.at[pl.ds(0, 8)], vs)
    arrive(brow.at[pl.ds(0, 6)], rs)

    @pl.when(y >= x)
    def _():
        arrive(fbuf.at[pl.ds(0, PLANES)], gs.at[1])
        arrive(brow.at[0], ts)

    arrive(racc.at[pl.ds(0, 17 * 8)], bs)


def by_planes(rows, ids, clus):
    vmem = pl.BlockSpec(memory_space=pltpu.VMEM)
    smem = pl.BlockSpec(memory_space=pltpu.SMEM)
    anywhere = pl.BlockSpec(memory_space=pl.ANY)
    dma = pltpu.SemaphoreType.DMA
    best = pl.pallas_call(
        plane_kernel,
        out_shape=jax.ShapeDtypeStruct((1, rows.shape[0]), F32),
        in_specs=[smem, vmem, anywhere],
        out_specs=vmem,
        scratch_shapes=[
            pltpu.VMEM(ids.shape, I32),
            pltpu.VMEM((PLANES * PIECE, D), BF16),
            pltpu.VMEM((PLANES * PIECE, D), BF16),
            pltpu.VMEM((PLANES * PIECE, D), BF16),
            pltpu.VMEM((PLANES * SIDE, PIECE, D), BF16),
            pltpu.VMEM((PLANES * SIDE, PIECE, D), BF16),
            pltpu.VMEM((PLANES * CHUNK, 128), F32),
            pltpu.VMEM((PIECE, 128), F32),
            pltpu.VMEM((PLANES * SIDE, 8, PIECE), F32),
            pltpu.VMEM((PLANES * SIDE, 8, PIECE), F32),
            pltpu.VMEM((SIDE, 8, 128), F32),
            pltpu.VMEM((SIDE, 8, 128), F32),
            pltpu.VMEM((SIDE, 8, 128), F32),
            pltpu.VMEM((SIDE, 8, 128), F32),
            pltpu.VMEM((SLOTS, 8, 128), F32),
            pltpu.VMEM((SLOTS, 8, 128), F32),
            pltpu.VMEM((PLANES, 8, 128), F32),
            pltpu.VMEM((PLANES, 8, 128), F32),
            dma, dma((PLANES,)),
            dma, dma((PLANES,)), dma((PLANES,)),
            dma((2,)), dma, dma((PLANES, 4)), dma((PLANES, 4)),
            dma, dma((2,)),
            dma, dma((3,)),
            dma, dma,
        ],
        compiler_params=pltpu.CompilerParams(
            collective_id=0, has_side_effects=True, vmem_limit_bytes=40 * 2**20
        ),
        name="by_planes",
    )(clus, rows, ids)
    return best.reshape(-1)


def shards(embeddings, member_rows, cluster_sizes, unit_pairs):
    rows, ids, clus, fits = prepare(embeddings, member_rows, cluster_sizes)
    return lax.cond(
        fits[0] > 0,
        lambda: by_planes(rows, ids, clus),
        lambda: direct(embeddings, member_rows, cluster_sizes, unit_pairs),
    )


def solution(mesh):
    placed = (P(AXES, None), P(), P(), P())
    return jax.shard_map(shards, mesh=mesh, in_specs=placed, out_specs=P(AXES), check_vma=False)
```

```python
import functools

import jax
import jax.numpy as jnp
from jax import lax
from jax.experimental import pallas as pl
from jax.experimental.pallas import tpu as pltpu
from jax.sharding import PartitionSpec as P

BLOCK = 256
GROUP_BLOCKS = 8
GROUP = BLOCK * GROUP_BLOCKS
AXES = ("store", "tile")
EPS = 1e-06
FLOOR = -4.0

MESH = pl.DeviceIdType.MESH
PLANES = 4
SIDE = 4
SLOTS = 8
SHARE = 16
PIECE = 8 * SHARE
CHUNK = SIDE * PIECE
HALF = PIECE // 2
D = 1024
BF16 = jnp.bfloat16
F32 = jnp.float32
I32 = jnp.int32


def compare_pair(left, right, same_group):
    span = 512

    def step(col_best, at):
        part = lax.dynamic_slice_in_dim(left, at, span)
        scores = lax.dot_general(part, right, (((1,), (1,)), ((), ())), preferred_element_type=F32)
        row_ids = at + lax.broadcasted_iota(I32, scores.shape, 0)
        col_ids = lax.broadcasted_iota(I32, scores.shape, 1)
        scores = jnp.where((row_ids == col_ids) & same_group, FLOOR, scores)
        return jnp.maximum(col_best, jnp.max(scores, axis=0)), jnp.max(scores, axis=1)

    first = jnp.full((right.shape[0],), FLOOR, F32)
    col_best, row_best = lax.scan(step, first, jnp.arange(0, left.shape[0], span, dtype=I32))
    return row_best.reshape(-1), col_best


def direct(embeddings, member_rows, cluster_sizes, unit_pairs):
    devices = lax.axis_size(AXES)
    me = lax.axis_index(AXES)
    rows_dev, width = embeddings.shape
    groups = member_rows.size // GROUP
    share = GROUP // devices
    owners = unit_pairs.shape[0]

    wide = embeddings.astype(F32)
    squares = jnp.sum(jnp.square(wide), axis=1, keepdims=True)
    unit = (wide * lax.rsqrt(squares + EPS)).astype(BF16)

    local = member_rows.reshape(-1, BLOCK) - me * rows_dev
    mine = (local >= 0) & (local < rows_dev)
    low = jnp.min(jnp.where(mine, local, rows_dev), axis=1)
    high = jnp.max(jnp.where(mine, local, -1), axis=1)
    order = jnp.stack([low, high], axis=1).reshape(rows_dev)
    pick = order[:, None] == jnp.arange(rows_dev, dtype=I32)[None, :]
    ordered = lax.dot_general(
        pick.astype(BF16), unit, (((1,), (0,)), ((), ())), preferred_element_type=F32
    ).astype(BF16)
    by_group = ordered.reshape(groups, share, width)

    first_group = (jnp.cumsum(cluster_sizes) - cluster_sizes) // GROUP
    pairs = unit_pairs[:, 0]
    usable = pairs[:, 0] >= 0
    sides = first_group[jnp.maximum(pairs[:, :1], 0)] + jnp.maximum(pairs[:, 1:], 0)
    outgoing = by_group[sides].reshape(owners, 2 * share, width)
    arrived = lax.all_to_all(outgoing, AXES, split_axis=0, concat_axis=0, tiled=True)
    arrived = arrived.reshape(devices, 2, share, width)
    left = arrived[:, 0].reshape(GROUP, width)
    right = arrived[:, 1].reshape(GROUP, width)
    row_best, col_best = compare_pair(left, right, sides[me, 0] == sides[me, 1])
    best = jnp.stack([row_best.reshape(devices, share), col_best.reshape(devices, share)], axis=1)
    best = jnp.where(usable[me], best, FLOOR).reshape(devices, 2 * share)
    back = lax.all_to_all(best, AXES, split_axis=0, concat_axis=0, tiled=True)
    back = back.reshape(owners * 2, share)
    of_group = sides.reshape(-1)[None, :] == jnp.arange(groups, dtype=I32)[:, None]
    best_slot = jnp.max(jnp.where(of_group[:, :, None], back[None], FLOOR), axis=1)
    return jnp.max(jnp.where(pick, best_slot.reshape(rows_dev, 1), FLOOR), axis=0)


def prepare_kernel(clusters, sizes_ref, emb_ref, members_ref, rows_ref, ids_ref, clus_ref, fits_ref, group_at, low_ref, high_ref, picked_ref):
    me = lax.axis_index("store") * (2 * SIDE * SIDE) + lax.axis_index("tile")
    rows_dev = emb_ref.shape[0]
    blocks = members_ref.shape[0] // 2
    local = [members_ref[pl.ds(h, blocks, stride=2), :] - me * rows_dev for h in range(2)]
    mine = [(part >= 0) & (part < rows_dev) for part in local]
    low = [jnp.where(ok, part, rows_dev) for ok, part in zip(mine, local)]
    high = [jnp.where(ok, part, -1) for ok, part in zip(mine, local)]
    low = jnp.min(jnp.minimum(*low), axis=1, keepdims=True)
    high = jnp.max(jnp.maximum(*high), axis=1, keepdims=True)
    low_ref[...] = jnp.broadcast_to(low, (blocks, 128))
    high_ref[...] = jnp.broadcast_to(high, (blocks, 128))
    wide = emb_ref[...].astype(F32)
    squares = jnp.sum(wide * wide, axis=1, keepdims=True)
    unit = (wide * lax.rsqrt(squares + EPS)).astype(BF16)
    column = lax.broadcasted_iota(I32, (blocks, rows_dev), 1)
    for h, wanted in enumerate((low, high)):
        pick = jnp.where(wanted == column, 1.0, 0.0).astype(BF16)
        picked_ref[h * blocks : (h + 1) * blocks, :] = lax.dot_general(
            pick, unit, (((1,), (0,)), ((), ())), preferred_element_type=F32
        )

    counts = [sizes_ref[c] // GROUP for c in range(clusters)]
    way = lax.broadcasted_iota(I32, (128, 128), 0) * 128 + lax.broadcasted_iota(I32, (128, 128), 1)
    loads = jnp.full((128, 128), counts[0], I32)
    for c in range(1, clusters):
        plane = lax.shift_right_logical(way, 2 * (c - 1)) & 3
        loads += lax.shift_left(jnp.full((128, 128), counts[c], I32), plane * 8)
    most = loads & 255
    for p in range(1, PLANES):
        most = jnp.maximum(most, lax.shift_right_logical(loads, 8 * p) & 255)
    chosen = jnp.min(most * 16384 + way)
    fits_ref[0] = (chosen // 16384 <= SLOTS).astype(I32)
    groups = PLANES * SLOTS
    for d in range(groups):
        group_at[d] = 0
        clus_ref[d] = -1
    used = [jnp.int32(0)] * PLANES
    start = jnp.int32(0)
    for c in range(clusters):
        plane = jnp.int32(0) if c == 0 else lax.shift_right_logical(chosen, 2 * (c - 1)) & 3
        offset = jnp.int32(0)
        for p in range(PLANES):
            offset = jnp.where(plane == p, used[p], offset)

        def put(i, carry, c=c, plane=plane, offset=offset, start=start):
            at = jnp.minimum(plane * SLOTS + offset + i, groups - 1)
            group_at[at] = jnp.minimum(start + i, groups - 1)
            clus_ref[at] = c
            return carry

        lax.fori_loop(0, counts[c], put, 0)
        for p in range(PLANES):
            used[p] = jnp.where(plane == p, used[p] + counts[c], used[p])
        start = start + counts[c]

    for d in range(groups):
        at = pl.multiple_of(group_at[d] * GROUP_BLOCKS, GROUP_BLOCKS)
        ids_ref[d * SHARE : d * SHARE + 8, :] = low_ref[pl.ds(at, 8), :]
        ids_ref[d * SHARE + 8 : d * SHARE + 16, :] = high_ref[pl.ds(at, 8), :]
        lower = picked_ref[pl.ds(at, 8), :]
        upper = picked_ref[pl.ds(pl.multiple_of(at + 256, 8), 8), :]
        rows_ref[d * SHARE : (d + 1) * SHARE, :] = jnp.concatenate([lower, upper], axis=0).astype(BF16)


def prepare(embeddings, member_rows, cluster_sizes):
    rows_dev, width = embeddings.shape
    vmem = pl.BlockSpec(memory_space=pltpu.VMEM)
    smem = pl.BlockSpec(memory_space=pltpu.SMEM)
    groups = PLANES * SLOTS
    return pl.pallas_call(
        functools.partial(prepare_kernel, cluster_sizes.shape[0]),
        out_shape=(
            jax.ShapeDtypeStruct((rows_dev, width), BF16),
            jax.ShapeDtypeStruct((rows_dev, 128), I32),
            jax.ShapeDtypeStruct((groups,), I32),
            jax.ShapeDtypeStruct((1,), I32),
        ),
        in_specs=[smem, vmem, vmem],
        out_specs=(vmem, vmem, smem, smem),
        scratch_shapes=[
            pltpu.SMEM((groups,), I32),
            pltpu.VMEM((member_rows.size // BLOCK, 128), I32),
            pltpu.VMEM((member_rows.size // BLOCK, 128), I32),
            pltpu.VMEM((rows_dev, width), F32),
        ],
        compiler_params=pltpu.CompilerParams(vmem_limit_bytes=32 * 2**20),
        name="prepare",
    )(cluster_sizes, embeddings, member_rows.reshape(-1, BLOCK // 2))


def plane_kernel(
    clus_ref, src, ids_hbm, out_ref,
    ids_ref, zbuf, erow, ecol, fbuf, hbuf, racc, hacc, cacc, fcacc, fsend, hsend,
    rrow, rcol, brow, bcol, zout, fin,
    zs, zr, es, er, ec, gs, vs, fr, hr,
    rs, rr, bs, br, ts, ids_sem,
):
    z = lax.axis_index("store")
    tile = lax.axis_index("tile")
    y, x, k = tile // 8, (tile // 2) % 4, tile % 2

    def far(from_, to, ssem, rsem, dz, dy, dx, dk):
        pltpu.make_async_remote_copy(
            from_, to, ssem, rsem, device_id=(dz, dy * 8 + dx * 2 + dk), device_id_type=MESH
        ).start()

    def near(from_, to, rsem):
        pltpu.make_async_copy(from_, to, rsem).start()

    def arrive(ref, sem):
        pltpu.make_async_copy(ref, ref, sem).wait()

    diagonal = y == x
    in_row, in_col = 2 * y + k, 2 * x + k

    barrier = pltpu.get_barrier_semaphore()

    def greet(dz, dy, dx, dk):
        pl.semaphore_signal(barrier, inc=1, device_id=(dz, dy * 8 + dx * 2 + dk), device_id_type=MESH)

    for n in range(1, 8):
        i = (in_row + n) & 7
        greet(z, i // 2, x, i & 1)
    for n in range(1, SIDE):
        for core in range(2):
            greet(z, y, (x + n) & 3, core)
        greet((z + n) & 3, y, x, k)
    pl.semaphore_wait(barrier, 7 + 6 + 3)

    def hop(c):
        return (0, 1, 3, 2)[c]

    def chunk(c):
        return pl.ds(c * PIECE if isinstance(c, int) else pl.multiple_of(c * PIECE, PIECE), PIECE)

    def exchange(c):
        if c:
            arrive(zbuf.at[chunk(c)], zr.at[c])
        row_at = pl.ds(pl.multiple_of(c * PIECE + in_row * SHARE, SHARE), SHARE)
        col_at = pl.ds(pl.multiple_of(c * PIECE + in_col * SHARE, SHARE), SHARE)

        def piece(i):
            if c:
                return zbuf.at[pl.ds(pl.multiple_of(c * PIECE + i * SHARE, SHARE), SHARE)]
            return src.at[pl.ds(pl.multiple_of(z * PIECE + i * SHARE, SHARE), SHARE)]

        for n in range(1, 8):
            i = (in_row + n) & 7
            far(piece(i), erow.at[row_at], es, er.at[c], z, i // 2, x, i & 1)
            i = (in_col + n) & 7
            far(piece(i), ecol.at[col_at], es, ec.at[c], z, y, i // 2, i & 1)
        near(piece(in_row), erow.at[row_at], er.at[c])
        near(piece(in_col), ecol.at[col_at], ec.at[c])

    def col_core(cy, member):
        return jnp.where(cy < x, member, 1 - member)

    member = col_core(y, k)

    def gather(c):
        arrive(erow.at[chunk(c)], er.at[c])
        arrive(ecol.at[chunk(c)], ec.at[c])
        mine, at = chunk(c), c * SIDE
        for way, n in enumerate((1, 3)):
            px, py = (x + n) & 3, (y + n) & 3
            far(erow.at[mine], fbuf.at[at + 1 + way], gs.at[0], fr.at[c, way], z, y, px, k)
            far(ecol.at[mine], hbuf.at[at + 1 + way], gs.at[0], hr.at[c, way], z, py, x, col_core(py, k))
        near(erow.at[mine], fbuf.at[at], fr.at[c, 2])

        @pl.when(y < x)
        def _():
            near(ecol.at[mine], hbuf.at[at], hr.at[c, 2])

        @pl.when(y >= x)
        def _():
            far(ecol.at[mine], hbuf.at[at], gs.at[1], hr.at[c, 2], z, y, x, 1 - k)

    def pass_on(c):
        for way, n in enumerate((1, 3)):
            part = pl.ds(way * HALF, HALF)
            px, py = (x + n) & 3, (y + n) & 3
            at, to = c * SIDE + 1 + way, c * SIDE + 3
            arrive(fbuf.at[at], fr.at[c, way])
            far(fbuf.at[at, part], fbuf.at[to, part], vs, fr.at[c, 3], z, y, px, k)
            arrive(hbuf.at[at], hr.at[c, way])
            far(hbuf.at[at, part], hbuf.at[to, part], vs, hr.at[c, 3], z, py, x, col_core(py, member))

    def settle(c, shares=(2, 3)):
        for sem in shares:
            arrive(fbuf.at[0], fr.at[c, sem])
            arrive(hbuf.at[0], hr.at[c, sem])

    for c in range(1, PLANES):
        to = (z - hop(c)) & 3
        far(src.at[chunk(to)], zbuf.at[chunk(c)], zs, zr.at[c], to, y, x, k)
    exchange(0)
    near(ids_hbm, ids_ref, ids_sem)
    gather(0)
    for ref in (racc, hacc, cacc, fcacc, fsend, hsend):
        ref[...] = jnp.full(ref.shape, FLOOR, F32)
    exchange(1)
    exchange(2)
    exchange(3)
    gather(1)
    pass_on(0)
    gather(2)
    pass_on(1)
    pass_on(2)
    gather(3)

    first_slot = 2 * y + k
    other_slot = 2 * x + member
    together = clus_ref[z * SLOTS + first_slot] == clus_ref[z * SLOTS + other_slot]

    def meet(left, i, rows, right, j, cols, col, ok=None, same=False, rowmax=None):
        a = left[pl.ds(i, rows)].reshape(rows * PIECE, D)
        b = right[pl.ds(j, cols)].reshape(cols * PIECE, D)
        scores = lax.dot_general(a, b, (((1,), (1,)), ((), ())), preferred_element_type=F32)
        if same:
            eye = lax.broadcasted_iota(I32, scores.shape, 0) == lax.broadcasted_iota(I32, scores.shape, 1)
            scores = jnp.where(eye, FLOOR, scores)
        over = scores[:, :PIECE]
        for n in range(1, cols):
            over = jnp.maximum(over, scores[:, n * PIECE : (n + 1) * PIECE])
        down = jnp.max(scores.reshape(rows * PIECE // 8, 8, cols * PIECE), axis=0)
        if ok is not None:
            over = jnp.where(ok, over, FLOOR)
            down = jnp.where(ok, down, FLOOR)
        at = pl.ds(i * PIECE if isinstance(i, int) else pl.multiple_of(i * PIECE, PIECE), rows * PIECE)
        if rowmax is None:
            racc[at, :] = jnp.maximum(racc[at, :], over)
        else:
            rowmax[...] = jnp.maximum(rowmax[...], over)
        for n in range(cols):
            col[j + n] = jnp.maximum(col[j + n], down[:, n * PIECE : (n + 1) * PIECE])

    off = jnp.logical_not(diagonal)

    def corner(i, rows, t):
        @pl.when(diagonal)
        def _():
            meet(fbuf, i, rows, fbuf, t * SIDE, SIDE, fcacc)

        @pl.when(off)
        def _():
            meet(fbuf, i, rows, hbuf, t * SIDE, SIDE, cacc, together)

        meet(fbuf, t * SIDE, SIDE, hbuf, i, rows, cacc, together)

    def middle(i, rows, takes):
        @pl.when(diagonal)
        def _():
            meet(fbuf, i, rows, fbuf, i, rows, fcacc, same=True)

        @pl.when(off | takes)
        def _():
            meet(fbuf, i, rows, hbuf, i, rows, cacc, together)

    def compute(c):
        def before(t, carry):
            corner(c * SIDE, SIDE, t)
            return carry

        lax.fori_loop(0, c, before, 0)
        middle(c * SIDE, SIDE, (k == 0) == (c < 2))

    def early(c, carry):
        settle(c)
        compute(c)
        return carry

    lax.fori_loop(0, 3, early, 0)
    pass_on(3)
    arrive(fbuf.at[pl.ds(0, 3)], zs)
    arrive(fbuf.at[pl.ds(0, 7)], es)
    arrive(fbuf, gs.at[0])

    last, takes = 3 * SIDE, k == 1
    settle(3, (2,))

    def ahead(t, carry):
        corner(last, 3, t)
        return carry

    lax.fori_loop(0, 3, ahead, 0)
    middle(last, 3, takes)
    def flat(s, c):
        at = (c * SIDE + s) * PIECE
        fsend[s, c : c + 1, :] = jnp.max(racc[at : at + PIECE, :].T, axis=0, keepdims=True)

    for s in range(SIDE):
        for c in range(PLANES):
            if (s, c) != (3, 3):
                flat(s, c)
    settle(3, (3,))

    @pl.when(off)
    def _():
        meet(fbuf, 15, 1, hbuf, 0, 16, cacc, together)
        meet(hbuf, 15, 1, fbuf, 0, 15, fcacc, together, rowmax=hacc)

    @pl.when(diagonal)
    def _():
        meet(fbuf, 15, 1, fbuf, 0, 15, fcacc)
        meet(fbuf, 15, 1, fbuf, 15, 1, fcacc, same=True)
        meet(hbuf, 15, 1, fbuf, 0, 12, fcacc, together, rowmax=hacc)

    @pl.when(diagonal & takes)
    def _():
        meet(fbuf, 15, 1, hbuf, 12, 4, cacc, together)
        meet(hbuf, 15, 1, fbuf, 12, 3, fcacc, together, rowmax=hacc)

    places = (0, 3, 1, 2)
    for s in (1, 2, 3, 0):
        for c in range(PLANES):
            best = jnp.max(cacc[c * SIDE + s], axis=0, keepdims=True)
            if (s, c) == (3, 3):
                best = jnp.maximum(best, jnp.max(hacc[...].T, axis=0, keepdims=True))
            hsend[s, c : c + 1, :] = best
        if s:
            far(hsend.at[s], rcol.at[y], rs, rr.at[1], z, (y + places[s]) & 3, x, member)

    @pl.when(y < x)
    def _():
        near(hsend.at[0], rcol.at[y], rr.at[1])

    @pl.when(y >= x)
    def _():
        far(hsend.at[0], rcol.at[y], ts, rr.at[1], z, y, x, 1 - k)

    flat(3, 3)
    for s in (1, 2, 3, 0):
        for c in range(PLANES):
            best = jnp.max(fcacc[c * SIDE + s], axis=0, keepdims=True)
            fsend[s, c : c + 1, :] = jnp.maximum(fsend[s, c : c + 1, :], best)
        if s:
            far(fsend.at[s], rrow.at[x], rs, rr.at[0], z, y, (x + places[s]) & 3, k)
        else:
            near(fsend.at[0], rrow.at[x], rr.at[0])

    def total(ref, sem):
        arrive(ref, sem)
        best = ref[0]
        for i in range(1, SIDE):
            best = jnp.maximum(best, ref[i])
        ref[0] = best

    total(rcol, rr.at[1])
    for n in range(1, 8):
        i = (in_col + n) & 7
        far(rcol.at[0], bcol.at[in_col], bs, br.at[1], z, y, i // 2, i & 1)
    near(rcol.at[0], bcol.at[in_col], br.at[1])
    total(rrow, rr.at[0])
    for n in range(1, 8):
        i = (in_row + n) & 7
        far(rrow.at[0], brow.at[in_row], bs, br.at[0], z, i // 2, x, i & 1)
    near(rrow.at[0], brow.at[in_row], br.at[0])
    arrive(fbuf.at[pl.ds(0, 8)], vs)
    arrive(racc.at[pl.ds(0, 6 * 8)], rs)

    @pl.when(y >= x)
    def _():
        arrive(fbuf.at[pl.ds(0, PLANES)], gs.at[1])
        arrive(racc.at[pl.ds(0, 8)], ts)

    arrive(ids_ref, ids_sem)
    arrive(brow, br.at[0])
    arrive(bcol, br.at[1])
    for c in range(PLANES):
        from_row = jnp.concatenate([brow[s, c : c + 1, :] for s in range(SLOTS)], axis=0)
        from_col = jnp.concatenate([bcol[s, c : c + 1, :] for s in range(SLOTS)], axis=0)
        from_row = pltpu.roll(from_row, (128 - in_row * SHARE) & 127, 1)
        from_col = pltpu.roll(from_col, (128 - in_col * SHARE) & 127, 1)
        value = jnp.maximum(from_row, from_col)
        if c:
            zout[c] = value
            far(zout.at[c], fin.at[c], bs, br.at[2], (z + hop(c)) & 3, y, x, k)
        else:
            fin[0] = value

    rows = PLANES * PIECE
    lane = lax.broadcasted_iota(I32, (PIECE, 128), 1)
    sub = lax.broadcasted_iota(I32, (PIECE, 128), 0) & (SHARE - 1)
    best = jnp.full((1, rows), FLOOR, F32)
    for c in range(PLANES):
        if c == 1:
            arrive(racc.at[pl.ds(0, 17 * 8)], bs)
            arrive(fin.at[pl.ds(1, 3)], br.at[2])
        spread = jnp.broadcast_to(fin[c].reshape(SLOTS, 1, 128), (SLOTS, SHARE, 128)).reshape(PIECE, 128)
        value = jnp.max(jnp.where(lane == sub, spread, FLOOR), axis=1, keepdims=True)
        pick = ids_ref[chunk((z - hop(c)) & 3), :][:, :1] == lax.broadcasted_iota(I32, (PIECE, rows), 1)
        best = jnp.maximum(best, jnp.max(jnp.where(pick, value, FLOOR), axis=0, keepdims=True))
    out_ref[...] = best


def by_planes(rows, ids, clus):
    vmem = pl.BlockSpec(memory_space=pltpu.VMEM)
    smem = pl.BlockSpec(memory_space=pltpu.SMEM)
    anywhere = pl.BlockSpec(memory_space=pl.ANY)
    dma = pltpu.SemaphoreType.DMA
    best = pl.pallas_call(
        plane_kernel,
        out_shape=jax.ShapeDtypeStruct((1, rows.shape[0]), F32),
        in_specs=[smem, vmem, anywhere],
        out_specs=vmem,
        scratch_shapes=[
            pltpu.VMEM(ids.shape, I32),
            pltpu.VMEM((PLANES * PIECE, D), BF16),
            pltpu.VMEM((PLANES * PIECE, D), BF16),
            pltpu.VMEM((PLANES * PIECE, D), BF16),
            pltpu.VMEM((PLANES * SIDE, PIECE, D), BF16),
            pltpu.VMEM((PLANES * SIDE, PIECE, D), BF16),
            pltpu.VMEM((PLANES * CHUNK, 128), F32),
            pltpu.VMEM((PIECE, 128), F32),
            pltpu.VMEM((PLANES * SIDE, 8, PIECE), F32),
            pltpu.VMEM((PLANES * SIDE, 8, PIECE), F32),
            pltpu.VMEM((SIDE, 8, 128), F32),
            pltpu.VMEM((SIDE, 8, 128), F32),
            pltpu.VMEM((SIDE, 8, 128), F32),
            pltpu.VMEM((SIDE, 8, 128), F32),
            pltpu.VMEM((SLOTS, 8, 128), F32),
            pltpu.VMEM((SLOTS, 8, 128), F32),
            pltpu.VMEM((PLANES, 8, 128), F32),
            pltpu.VMEM((PLANES, 8, 128), F32),
            dma, dma((PLANES,)),
            dma, dma((PLANES,)), dma((PLANES,)),
            dma((2,)), dma, dma((PLANES, 4)), dma((PLANES, 4)),
            dma, dma((2,)),
            dma, dma((3,)),
            dma, dma,
        ],
        compiler_params=pltpu.CompilerParams(
            collective_id=0, has_side_effects=True, vmem_limit_bytes=40 * 2**20
        ),
        name="by_planes",
    )(clus, rows, ids)
    return best.reshape(-1)


def shards(embeddings, member_rows, cluster_sizes, unit_pairs):
    rows, ids, clus, fits = prepare(embeddings, member_rows, cluster_sizes)
    return lax.cond(
        fits[0] > 0,
        lambda: by_planes(rows, ids, clus),
        lambda: direct(embeddings, member_rows, cluster_sizes, unit_pairs),
    )


def solution(mesh):
    placed = (P(AXES, None), P(), P(), P())
    return jax.shard_map(shards, mesh=mesh, in_specs=placed, out_specs=P(AXES), check_vma=False)
```

```python
import functools

import jax
import jax.numpy as jnp
from jax import lax
from jax.experimental import pallas as pl
from jax.experimental.pallas import tpu as pltpu
from jax.sharding import PartitionSpec as P

BLOCK = 256
GROUP_BLOCKS = 8
GROUP = BLOCK * GROUP_BLOCKS
AXES = ("store", "tile")
EPS = 1e-06
FLOOR = -4.0

MESH = pl.DeviceIdType.MESH
PLANES = 4
SIDE = 4
SLOTS = 8
SHARE = 16
PIECE = 8 * SHARE
CHUNK = SIDE * PIECE
HALF = PIECE // 2
D = 1024
BF16 = jnp.bfloat16
F32 = jnp.float32
I32 = jnp.int32


def compare_pair(left, right, same_group):
    span = 512

    def step(col_best, at):
        part = lax.dynamic_slice_in_dim(left, at, span)
        scores = lax.dot_general(part, right, (((1,), (1,)), ((), ())), preferred_element_type=F32)
        row_ids = at + lax.broadcasted_iota(I32, scores.shape, 0)
        col_ids = lax.broadcasted_iota(I32, scores.shape, 1)
        scores = jnp.where((row_ids == col_ids) & same_group, FLOOR, scores)
        return jnp.maximum(col_best, jnp.max(scores, axis=0)), jnp.max(scores, axis=1)

    first = jnp.full((right.shape[0],), FLOOR, F32)
    col_best, row_best = lax.scan(step, first, jnp.arange(0, left.shape[0], span, dtype=I32))
    return row_best.reshape(-1), col_best


def direct(embeddings, member_rows, cluster_sizes, unit_pairs):
    devices = lax.axis_size(AXES)
    me = lax.axis_index(AXES)
    rows_dev, width = embeddings.shape
    groups = member_rows.size // GROUP
    share = GROUP // devices
    owners = unit_pairs.shape[0]

    wide = embeddings.astype(F32)
    squares = jnp.sum(jnp.square(wide), axis=1, keepdims=True)
    unit = (wide * lax.rsqrt(squares + EPS)).astype(BF16)

    local = member_rows.reshape(-1, BLOCK) - me * rows_dev
    mine = (local >= 0) & (local < rows_dev)
    low = jnp.min(jnp.where(mine, local, rows_dev), axis=1)
    high = jnp.max(jnp.where(mine, local, -1), axis=1)
    order = jnp.stack([low, high], axis=1).reshape(rows_dev)
    pick = order[:, None] == jnp.arange(rows_dev, dtype=I32)[None, :]
    ordered = lax.dot_general(
        pick.astype(BF16), unit, (((1,), (0,)), ((), ())), preferred_element_type=F32
    ).astype(BF16)
    by_group = ordered.reshape(groups, share, width)

    first_group = (jnp.cumsum(cluster_sizes) - cluster_sizes) // GROUP
    pairs = unit_pairs[:, 0]
    usable = pairs[:, 0] >= 0
    sides = first_group[jnp.maximum(pairs[:, :1], 0)] + jnp.maximum(pairs[:, 1:], 0)
    outgoing = by_group[sides].reshape(owners, 2 * share, width)
    arrived = lax.all_to_all(outgoing, AXES, split_axis=0, concat_axis=0, tiled=True)
    arrived = arrived.reshape(devices, 2, share, width)
    left = arrived[:, 0].reshape(GROUP, width)
    right = arrived[:, 1].reshape(GROUP, width)
    row_best, col_best = compare_pair(left, right, sides[me, 0] == sides[me, 1])
    best = jnp.stack([row_best.reshape(devices, share), col_best.reshape(devices, share)], axis=1)
    best = jnp.where(usable[me], best, FLOOR).reshape(devices, 2 * share)
    back = lax.all_to_all(best, AXES, split_axis=0, concat_axis=0, tiled=True)
    back = back.reshape(owners * 2, share)
    of_group = sides.reshape(-1)[None, :] == jnp.arange(groups, dtype=I32)[:, None]
    best_slot = jnp.max(jnp.where(of_group[:, :, None], back[None], FLOOR), axis=1)
    return jnp.max(jnp.where(pick, best_slot.reshape(rows_dev, 1), FLOOR), axis=0)


def prepare_kernel(clusters, sizes_ref, emb_ref, members_ref, rows_ref, ids_ref, clus_ref, fits_ref, group_at, low_ref, high_ref, picked_ref):
    me = lax.axis_index("store") * (2 * SIDE * SIDE) + lax.axis_index("tile")
    rows_dev = emb_ref.shape[0]
    blocks = members_ref.shape[0] // 2
    local = [members_ref[pl.ds(h, blocks, stride=2), :] - me * rows_dev for h in range(2)]
    mine = [(part >= 0) & (part < rows_dev) for part in local]
    low = [jnp.where(ok, part, rows_dev) for ok, part in zip(mine, local)]
    high = [jnp.where(ok, part, -1) for ok, part in zip(mine, local)]
    low = jnp.min(jnp.minimum(*low), axis=1, keepdims=True)
    high = jnp.max(jnp.maximum(*high), axis=1, keepdims=True)
    low_ref[...] = jnp.broadcast_to(low, (blocks, 128))
    high_ref[...] = jnp.broadcast_to(high, (blocks, 128))
    wide = emb_ref[...].astype(F32)
    squares = jnp.sum(wide * wide, axis=1, keepdims=True)
    unit = (wide * lax.rsqrt(squares + EPS)).astype(BF16)
    column = lax.broadcasted_iota(I32, (blocks, rows_dev), 1)
    for h, wanted in enumerate((low, high)):
        pick = jnp.where(wanted == column, 1.0, 0.0).astype(BF16)
        picked_ref[h * blocks : (h + 1) * blocks, :] = lax.dot_general(
            pick, unit, (((1,), (0,)), ((), ())), preferred_element_type=F32
        )

    counts = [sizes_ref[c] // GROUP for c in range(clusters)]
    way = lax.broadcasted_iota(I32, (128, 128), 0) * 128 + lax.broadcasted_iota(I32, (128, 128), 1)
    loads = jnp.full((128, 128), counts[0], I32)
    for c in range(1, clusters):
        plane = lax.shift_right_logical(way, 2 * (c - 1)) & 3
        loads += lax.shift_left(jnp.full((128, 128), counts[c], I32), plane * 8)
    most = loads & 255
    for p in range(1, PLANES):
        most = jnp.maximum(most, lax.shift_right_logical(loads, 8 * p) & 255)
    chosen = jnp.min(most * 16384 + way)
    fits_ref[0] = (chosen // 16384 <= SLOTS).astype(I32)
    groups = PLANES * SLOTS
    for d in range(groups):
        group_at[d] = 0
        clus_ref[d] = -1
    used = [jnp.int32(0)] * PLANES
    start = jnp.int32(0)
    for c in range(clusters):
        plane = jnp.int32(0) if c == 0 else lax.shift_right_logical(chosen, 2 * (c - 1)) & 3
        offset = jnp.int32(0)
        for p in range(PLANES):
            offset = jnp.where(plane == p, used[p], offset)

        def put(i, carry, c=c, plane=plane, offset=offset, start=start):
            at = jnp.minimum(plane * SLOTS + offset + i, groups - 1)
            group_at[at] = jnp.minimum(start + i, groups - 1)
            clus_ref[at] = c
            return carry

        lax.fori_loop(0, counts[c], put, 0)
        for p in range(PLANES):
            used[p] = jnp.where(plane == p, used[p] + counts[c], used[p])
        start = start + counts[c]

    for d in range(groups):
        at = pl.multiple_of(group_at[d] * GROUP_BLOCKS, GROUP_BLOCKS)
        ids_ref[d * SHARE : d * SHARE + 8, :] = low_ref[pl.ds(at, 8), :]
        ids_ref[d * SHARE + 8 : d * SHARE + 16, :] = high_ref[pl.ds(at, 8), :]
        lower = picked_ref[pl.ds(at, 8), :]
        upper = picked_ref[pl.ds(pl.multiple_of(at + 256, 8), 8), :]
        rows_ref[d * SHARE : (d + 1) * SHARE, :] = jnp.concatenate([lower, upper], axis=0).astype(BF16)


def prepare(embeddings, member_rows, cluster_sizes):
    rows_dev, width = embeddings.shape
    vmem = pl.BlockSpec(memory_space=pltpu.VMEM)
    smem = pl.BlockSpec(memory_space=pltpu.SMEM)
    groups = PLANES * SLOTS
    return pl.pallas_call(
        functools.partial(prepare_kernel, cluster_sizes.shape[0]),
        out_shape=(
            jax.ShapeDtypeStruct((rows_dev, width), BF16),
            jax.ShapeDtypeStruct((rows_dev, 128), I32),
            jax.ShapeDtypeStruct((groups,), I32),
            jax.ShapeDtypeStruct((1,), I32),
        ),
        in_specs=[smem, vmem, vmem],
        out_specs=(vmem, vmem, smem, smem),
        scratch_shapes=[
            pltpu.SMEM((groups,), I32),
            pltpu.VMEM((member_rows.size // BLOCK, 128), I32),
            pltpu.VMEM((member_rows.size // BLOCK, 128), I32),
            pltpu.VMEM((rows_dev, width), F32),
        ],
        compiler_params=pltpu.CompilerParams(vmem_limit_bytes=32 * 2**20),
        name="prepare",
    )(cluster_sizes, embeddings, member_rows.reshape(-1, BLOCK // 2))


def plane_kernel(
    clus_ref, src, ids_hbm, out_ref,
    ids_ref, zbuf, erow, ecol, fbuf, hbuf, racc, hacc, cacc, fcacc, fsend, hsend,
    rrow, rcol, brow, bcol, zout, fin,
    zs, zr, es, er, ec, gs, vs, fr, hr,
    rs, rr, bs, br, ts, ids_sem,
):
    z = lax.axis_index("store")
    tile = lax.axis_index("tile")
    y, x, k = tile // 8, (tile // 2) % 4, tile % 2

    def far(from_, to, ssem, rsem, dz, dy, dx, dk):
        pltpu.make_async_remote_copy(
            from_, to, ssem, rsem, device_id=(dz, dy * 8 + dx * 2 + dk), device_id_type=MESH
        ).start()

    def near(from_, to, rsem):
        pltpu.make_async_copy(from_, to, rsem).start()

    def arrive(ref, sem):
        pltpu.make_async_copy(ref, ref, sem).wait()

    diagonal = y == x
    in_row, in_col = 2 * y + k, 2 * x + k

    barrier = pltpu.get_barrier_semaphore()

    def greet(dz, dy, dx, dk):
        pl.semaphore_signal(barrier, inc=1, device_id=(dz, dy * 8 + dx * 2 + dk), device_id_type=MESH)

    for n in range(1, 8):
        i = (in_row + n) & 7
        greet(z, i // 2, x, i & 1)
    for n in range(1, SIDE):
        for core in range(2):
            greet(z, y, (x + n) & 3, core)
        greet((z + n) & 3, y, x, k)
    pl.semaphore_wait(barrier, 7 + 6 + 3)

    def hop(c):
        return (0, 1, 3, 2)[c]

    def chunk(c):
        return pl.ds(c * PIECE if isinstance(c, int) else pl.multiple_of(c * PIECE, PIECE), PIECE)

    def exchange(c):
        if c:
            arrive(zbuf.at[chunk(c)], zr.at[c])
        row_at = pl.ds(pl.multiple_of(c * PIECE + in_row * SHARE, SHARE), SHARE)
        col_at = pl.ds(pl.multiple_of(c * PIECE + in_col * SHARE, SHARE), SHARE)

        def piece(i):
            if c:
                return zbuf.at[pl.ds(pl.multiple_of(c * PIECE + i * SHARE, SHARE), SHARE)]
            return src.at[pl.ds(pl.multiple_of(z * PIECE + i * SHARE, SHARE), SHARE)]

        for n in range(1, 8):
            i = (in_row + n) & 7
            far(piece(i), erow.at[row_at], es, er.at[c], z, i // 2, x, i & 1)
            i = (in_col + n) & 7
            far(piece(i), ecol.at[col_at], es, ec.at[c], z, y, i // 2, i & 1)
        near(piece(in_row), erow.at[row_at], er.at[c])
        near(piece(in_col), ecol.at[col_at], ec.at[c])

    def col_core(cy, member):
        return jnp.where(cy < x, member, 1 - member)

    member = col_core(y, k)

    def gather(c):
        arrive(erow.at[chunk(c)], er.at[c])
        arrive(ecol.at[chunk(c)], ec.at[c])
        mine, at = chunk(c), c * SIDE
        for way, n in enumerate((1, 3)):
            px, py = (x + n) & 3, (y + n) & 3
            far(erow.at[mine], fbuf.at[at + 1 + way], gs.at[0], fr.at[c, way], z, y, px, k)
            far(ecol.at[mine], hbuf.at[at + 1 + way], gs.at[0], hr.at[c, way], z, py, x, col_core(py, k))
        near(erow.at[mine], fbuf.at[at], fr.at[c, 2])

        @pl.when(y < x)
        def _():
            near(ecol.at[mine], hbuf.at[at], hr.at[c, 2])

        @pl.when(y >= x)
        def _():
            far(ecol.at[mine], hbuf.at[at], gs.at[1], hr.at[c, 2], z, y, x, 1 - k)

    def pass_on(c):
        for way, n in enumerate((1, 3)):
            part = pl.ds(way * HALF, HALF)
            px, py = (x + n) & 3, (y + n) & 3
            at, to = c * SIDE + 1 + way, c * SIDE + 3
            arrive(fbuf.at[at], fr.at[c, way])
            far(fbuf.at[at, part], fbuf.at[to, part], vs, fr.at[c, 3], z, y, px, k)
            arrive(hbuf.at[at], hr.at[c, way])
            far(hbuf.at[at, part], hbuf.at[to, part], vs, hr.at[c, 3], z, py, x, col_core(py, member))

    def settle(c, shares=(2, 3)):
        for sem in shares:
            arrive(fbuf.at[0], fr.at[c, sem])
            arrive(hbuf.at[0], hr.at[c, sem])

    for c in range(1, PLANES):
        to = (z - hop(c)) & 3
        far(src.at[chunk(to)], zbuf.at[chunk(c)], zs, zr.at[c], to, y, x, k)
    exchange(0)
    near(ids_hbm, ids_ref, ids_sem)
    gather(0)
    for ref in (racc, hacc, cacc, fcacc, fsend, hsend):
        ref[...] = jnp.full(ref.shape, FLOOR, F32)
    exchange(1)
    exchange(2)
    exchange(3)
    gather(1)
    gather(2)
    pass_on(0)
    pass_on(1)
    pass_on(2)
    gather(3)

    first_slot = 2 * y + k
    other_slot = 2 * x + member
    together = clus_ref[z * SLOTS + first_slot] == clus_ref[z * SLOTS + other_slot]

    def meet(left, i, rows, right, j, cols, col, ok=None, same=False, rowmax=None):
        a = left[pl.ds(i, rows)].reshape(rows * PIECE, D)
        b = right[pl.ds(j, cols)].reshape(cols * PIECE, D)
        scores = lax.dot_general(a, b, (((1,), (1,)), ((), ())), preferred_element_type=F32)
        if same:
            eye = lax.broadcasted_iota(I32, scores.shape, 0) == lax.broadcasted_iota(I32, scores.shape, 1)
            scores = jnp.where(eye, FLOOR, scores)
        over = scores[:, :PIECE]
        for n in range(1, cols):
            over = jnp.maximum(over, scores[:, n * PIECE : (n + 1) * PIECE])
        down = jnp.max(scores.reshape(rows * PIECE // 8, 8, cols * PIECE), axis=0)
        if ok is not None:
            over = jnp.where(ok, over, FLOOR)
            down = jnp.where(ok, down, FLOOR)
        at = pl.ds(i * PIECE if isinstance(i, int) else pl.multiple_of(i * PIECE, PIECE), rows * PIECE)
        if rowmax is None:
            racc[at, :] = jnp.maximum(racc[at, :], over)
        else:
            rowmax[...] = jnp.maximum(rowmax[...], over)
        for n in range(cols):
            col[j + n] = jnp.maximum(col[j + n], down[:, n * PIECE : (n + 1) * PIECE])

    off = jnp.logical_not(diagonal)

    def corner(i, rows, t):
        @pl.when(diagonal)
        def _():
            meet(fbuf, i, rows, fbuf, t * SIDE, SIDE, fcacc)

        @pl.when(off)
        def _():
            meet(fbuf, i, rows, hbuf, t * SIDE, SIDE, cacc, together)

        meet(fbuf, t * SIDE, SIDE, hbuf, i, rows, cacc, together)

    def middle(i, rows, takes):
        @pl.when(diagonal)
        def _():
            meet(fbuf, i, rows, fbuf, i, rows, fcacc, same=True)

        @pl.when(off | takes)
        def _():
            meet(fbuf, i, rows, hbuf, i, rows, cacc, together)

    def compute(c):
        def before(t, carry):
            corner(c * SIDE, SIDE, t)
            return carry

        lax.fori_loop(0, c, before, 0)
        middle(c * SIDE, SIDE, (k == 0) == (c < 2))

    def early(c, carry):
        settle(c)
        compute(c)
        return carry

    lax.fori_loop(0, 3, early, 0)
    pass_on(3)
    arrive(fbuf.at[pl.ds(0, 3)], zs)
    arrive(fbuf.at[pl.ds(0, 7)], es)
    arrive(fbuf, gs.at[0])

    last, takes = 3 * SIDE, k == 1
    settle(3, (2,))

    def ahead(t, carry):
        corner(last, 3, t)
        return carry

    lax.fori_loop(0, 3, ahead, 0)
    middle(last, 3, takes)
    def flat(s, c):
        at = (c * SIDE + s) * PIECE
        fsend[s, c : c + 1, :] = jnp.max(racc[at : at + PIECE, :].T, axis=0, keepdims=True)

    for s in range(SIDE):
        for c in range(PLANES):
            if (s, c) != (3, 3):
                flat(s, c)
    settle(3, (3,))

    @pl.when(off)
    def _():
        meet(fbuf, 15, 1, hbuf, 0, 16, cacc, together)
        meet(hbuf, 15, 1, fbuf, 0, 15, fcacc, together, rowmax=hacc)

    @pl.when(diagonal)
    def _():
        meet(fbuf, 15, 1, fbuf, 0, 15, fcacc)
        meet(fbuf, 15, 1, fbuf, 15, 1, fcacc, same=True)
        meet(hbuf, 15, 1, fbuf, 0, 12, fcacc, together, rowmax=hacc)

    @pl.when(diagonal & takes)
    def _():
        meet(fbuf, 15, 1, hbuf, 12, 4, cacc, together)
        meet(hbuf, 15, 1, fbuf, 12, 3, fcacc, together, rowmax=hacc)

    places = (0, 3, 1, 2)
    for s in (1, 2, 3, 0):
        for c in range(PLANES):
            best = jnp.max(cacc[c * SIDE + s], axis=0, keepdims=True)
            if (s, c) == (3, 3):
                best = jnp.maximum(best, jnp.max(hacc[...].T, axis=0, keepdims=True))
            hsend[s, c : c + 1, :] = best
        if s:
            far(hsend.at[s], rcol.at[y], rs, rr.at[1], z, (y + places[s]) & 3, x, member)

    @pl.when(y < x)
    def _():
        near(hsend.at[0], rcol.at[y], rr.at[1])

    @pl.when(y >= x)
    def _():
        far(hsend.at[0], rcol.at[y], ts, rr.at[1], z, y, x, 1 - k)

    flat(3, 3)
    for s in (1, 2, 3, 0):
        for c in range(PLANES):
            best = jnp.max(fcacc[c * SIDE + s], axis=0, keepdims=True)
            fsend[s, c : c + 1, :] = jnp.maximum(fsend[s, c : c + 1, :], best)
        if s:
            far(fsend.at[s], rrow.at[x], rs, rr.at[0], z, y, (x + places[s]) & 3, k)
        else:
            near(fsend.at[0], rrow.at[x], rr.at[0])

    def total(ref, sem):
        arrive(ref, sem)
        best = ref[0]
        for i in range(1, SIDE):
            best = jnp.maximum(best, ref[i])
        ref[0] = best

    total(rcol, rr.at[1])
    for n in range(1, 8):
        i = (in_col + n) & 7
        far(rcol.at[0], bcol.at[in_col], bs, br.at[1], z, y, i // 2, i & 1)
    near(rcol.at[0], bcol.at[in_col], br.at[1])
    total(rrow, rr.at[0])
    for n in range(1, 8):
        i = (in_row + n) & 7
        far(rrow.at[0], brow.at[in_row], bs, br.at[0], z, i // 2, x, i & 1)
    near(rrow.at[0], brow.at[in_row], br.at[0])
    arrive(fbuf.at[pl.ds(0, 8)], vs)
    arrive(racc.at[pl.ds(0, 6 * 8)], rs)

    @pl.when(y >= x)
    def _():
        arrive(fbuf.at[pl.ds(0, PLANES)], gs.at[1])
        arrive(racc.at[pl.ds(0, 8)], ts)

    arrive(ids_ref, ids_sem)
    arrive(brow, br.at[0])
    arrive(bcol, br.at[1])
    for c in range(PLANES):
        from_row = jnp.concatenate([brow[s, c : c + 1, :] for s in range(SLOTS)], axis=0)
        from_col = jnp.concatenate([bcol[s, c : c + 1, :] for s in range(SLOTS)], axis=0)
        from_row = pltpu.roll(from_row, (128 - in_row * SHARE) & 127, 1)
        from_col = pltpu.roll(from_col, (128 - in_col * SHARE) & 127, 1)
        value = jnp.maximum(from_row, from_col)
        if c:
            zout[c] = value
            far(zout.at[c], fin.at[c], bs, br.at[2], (z + hop(c)) & 3, y, x, k)
        else:
            fin[0] = value

    rows = PLANES * PIECE
    lane = lax.broadcasted_iota(I32, (PIECE, 128), 1)
    sub = lax.broadcasted_iota(I32, (PIECE, 128), 0) & (SHARE - 1)
    best = jnp.full((1, rows), FLOOR, F32)
    for c in range(PLANES):
        if c == 1:
            arrive(racc.at[pl.ds(0, 17 * 8)], bs)
            arrive(fin.at[pl.ds(1, 3)], br.at[2])
        spread = jnp.broadcast_to(fin[c].reshape(SLOTS, 1, 128), (SLOTS, SHARE, 128)).reshape(PIECE, 128)
        value = jnp.max(jnp.where(lane == sub, spread, FLOOR), axis=1, keepdims=True)
        pick = ids_ref[chunk((z - hop(c)) & 3), :][:, :1] == lax.broadcasted_iota(I32, (PIECE, rows), 1)
        best = jnp.maximum(best, jnp.max(jnp.where(pick, value, FLOOR), axis=0, keepdims=True))
    out_ref[...] = best


def by_planes(rows, ids, clus):
    vmem = pl.BlockSpec(memory_space=pltpu.VMEM)
    smem = pl.BlockSpec(memory_space=pltpu.SMEM)
    anywhere = pl.BlockSpec(memory_space=pl.ANY)
    dma = pltpu.SemaphoreType.DMA
    best = pl.pallas_call(
        plane_kernel,
        out_shape=jax.ShapeDtypeStruct((1, rows.shape[0]), F32),
        in_specs=[smem, vmem, anywhere],
        out_specs=vmem,
        scratch_shapes=[
            pltpu.VMEM(ids.shape, I32),
            pltpu.VMEM((PLANES * PIECE, D), BF16),
            pltpu.VMEM((PLANES * PIECE, D), BF16),
            pltpu.VMEM((PLANES * PIECE, D), BF16),
            pltpu.VMEM((PLANES * SIDE, PIECE, D), BF16),
            pltpu.VMEM((PLANES * SIDE, PIECE, D), BF16),
            pltpu.VMEM((PLANES * CHUNK, 128), F32),
            pltpu.VMEM((PIECE, 128), F32),
            pltpu.VMEM((PLANES * SIDE, 8, PIECE), F32),
            pltpu.VMEM((PLANES * SIDE, 8, PIECE), F32),
            pltpu.VMEM((SIDE, 8, 128), F32),
            pltpu.VMEM((SIDE, 8, 128), F32),
            pltpu.VMEM((SIDE, 8, 128), F32),
            pltpu.VMEM((SIDE, 8, 128), F32),
            pltpu.VMEM((SLOTS, 8, 128), F32),
            pltpu.VMEM((SLOTS, 8, 128), F32),
            pltpu.VMEM((PLANES, 8, 128), F32),
            pltpu.VMEM((PLANES, 8, 128), F32),
            dma, dma((PLANES,)),
            dma, dma((PLANES,)), dma((PLANES,)),
            dma((2,)), dma, dma((PLANES, 4)), dma((PLANES, 4)),
            dma, dma((2,)),
            dma, dma((3,)),
            dma, dma,
        ],
        compiler_params=pltpu.CompilerParams(
            collective_id=0, has_side_effects=True, vmem_limit_bytes=40 * 2**20
        ),
        name="by_planes",
    )(clus, rows, ids)
    return best.reshape(-1)


def shards(embeddings, member_rows, cluster_sizes, unit_pairs):
    rows, ids, clus, fits = prepare(embeddings, member_rows, cluster_sizes)
    return lax.cond(
        fits[0] > 0,
        lambda: by_planes(rows, ids, clus),
        lambda: direct(embeddings, member_rows, cluster_sizes, unit_pairs),
    )


def solution(mesh):
    placed = (P(AXES, None), P(), P(), P())
    return jax.shard_map(shards, mesh=mesh, in_specs=placed, out_specs=P(AXES), check_vma=False)
```
